32 devices in a mesh: dp: 8 (over y, x, core), tensor: 4 (over z).
Axes of the slice: x: 2, y: 2, z: 4, core: 2. Of those that a mesh axis runs over, the one named last changes fastest.
Arguments:
- tokens: bfloat16 [192, 8192], P('dp', 'tensor'), may hold values from -6 to 6
- gate_weight: bfloat16 [8192, 28672], P('tensor', 'dp'), may hold values from -0.0625 to 0.0625
- up_weight: bfloat16 [8192, 28672], P('tensor', 'dp'), may hold values from -0.0625 to 0.0625
- down_weight: bfloat16 [28672, 8192], P('dp', 'tensor'), may hold values from -0.03125 to 0.03125
- adapter_proj_in: bfloat16 [256, 32, 8192], P('dp', None, 'tensor'), may hold values from -0.0625 to 0.0625
- adapter_lift_in: bfloat16 [256, 2, 16, 28672], P('tensor', None, None, 'dp'), may hold values from -1.5 to 1.5
- adapter_proj_out: bfloat16 [256, 16, 28672], P('tensor', None, 'dp'), may hold values from -0.03125 to 0.03125
- adapter_lift_out: bfloat16 [256, 16, 8192], P('dp', None, 'tensor'), may hold values from -1.5 to 1.5
- token_request: int32 [192], replicated, may hold values from 0 to 31, never falling along the last dimension, each value on 1 to 12 neighbouring positions
- request_adapter: int32 [32], replicated, may hold values from 0 to 255
- adapter_slot: int32 [256], replicated, may hold values from 0 to 255, each once
Outputs:
- mixed: bfloat16 [192, 8192], P('dp', 'tensor')
The draws below stay inside these ranges and needn't reach their ends.
Inputs may be any that keep to these rules, and one draw needn't show every extreme that they name: `token_request`: request numbers never fall along the tokens; every request has one or more tokens. `adapter_slot`: every slot holds exactly one adapter.
All inputs are finite; a program needn't handle non-finite values.
Results may differ from the reference program's by a relative error of at most 0.02.
Values may be sent and summed in bfloat16 or wider, within the bound.
No kernel may reach another device: no remote copies, remote signals or barrier semaphores. Data moves between devices by JAX's collectives and lax.ppermute only.
A program may use at most 192 MiB of HBM per device.

```python
import math
import jax
import jax.numpy as jnp
import numpy as np
from jax import lax

D = 8192
FF = 28672
R = 16
NADAPT = 256
TOK_DEV = 24
REQ_DEV = 4
TOKENS = 192
NREQ = 32
N_DP = 8
N_TENSOR = 4


def with_ends(entries, stream_key, least, high):
    spot = [jax.random.randint(jax.random.fold_in(stream_key, axis), (), 0, length) for axis, length in enumerate(entries.shape)]
    longest = entries.shape.index(max(entries.shape))
    beside = spot[:longest] + [(spot[longest] + 1) % entries.shape[longest]] + spot[longest + 1:]
    return entries.at[tuple(spot)].set(least).at[tuple(beside)].set(high)


def block_levels(rng, dims, shards, low, high):
    level = 1.0
    for dim, blocks in shards:
        steps = jax.random.uniform(jax.random.fold_in(jax.random.fold_in(rng, 6), dim), (blocks,), jnp.float32, low / len(shards), high / len(shards))
        level = level * jnp.repeat(jnp.exp(steps), dims[dim] // blocks).reshape((-1,) + (1,) * (len(dims) - 1 - dim))
    return level


def rank_bounds(count, slope):
    portions = [(1 << 20) // math.isqrt(rank ** slope) + 1 for rank in range(1, count + 1)]
    deviation = 1 + sum(portions) // (1 << 30)
    return np.cumsum(np.array([max(1, weight // deviation) for weight in portions]))


def skewed_ids(rng, dims, amount, skew):
    table = rank_bounds(amount, skew)
    ticket = jax.random.randint(jax.random.fold_in(rng, 1), dims, 0, int(table[amount - 1]))
    rank = jnp.searchsorted(jnp.asarray(table, jnp.int32), ticket, side="right")
    return jax.random.permutation(jax.random.fold_in(rng, 2), amount)[rank].astype(jnp.int32)


def length_profile(count, total, reach, lean):
    portions = [(1 << 20) // math.isqrt(grade ** lean) + 1 for grade in range(2, count + 1)]
    surplus, counts = total - reach - (count - 1), [1] * (count - 1)
    while surplus > 0:
        movable = [i for i in range(count - 1) if counts[i] < reach]
        pool, remaining = sum([portions[i] for i in movable]), surplus
        for i in movable:
            extra = min(reach - counts[i], max(1, remaining * portions[i] // pool), surplus)
            counts[i] = counts[i] + extra
            surplus = surplus - extra
    return np.array([reach] + counts)


def uneven_parts(rng, number_of, total, limit, slope):
    if number_of == 2:
        one = jax.random.randint(rng, (), max(1, total - limit), min(limit, total - 1) + 1)
        return jnp.stack([one, total - one])
    sizes = jnp.asarray(length_profile(number_of, total, limit, slope), jnp.int32)
    pairs = (number_of - 1) // 2
    source_of, receiver = sizes[1:1 + 2 * pairs:2], sizes[2:2 + 2 * pairs:2]
    slack = jnp.minimum(source_of - 1, limit - receiver)
    passed = jax.random.randint(jax.random.fold_in(rng, 1), (pairs,), 0, 1 << 20) % (slack + 1)
    sizes = sizes.at[1:1 + 2 * pairs:2].set(source_of - passed).at[2:2 + 2 * pairs:2].set(receiver + passed)
    return sizes[jax.random.permutation(jax.random.fold_in(rng, 2), number_of)]


def noise(key, extent, deviation, reach, pieces=(), kind=jnp.bfloat16):
    array = deviation * jax.random.normal(key, extent, jnp.float32)
    if pieces:
        array = array * block_levels(key, extent, pieces, -0.22, 0.18)
    return jnp.clip(array, -reach, reach).astype(kind)


def setup_inputs(seed: int = 0) -> dict:
    key_list = jax.random.split(jax.random.key(seed), 12)
    tokens = noise(key_list[0], (TOKENS, D), 1.0, 6.0, ((0, 8), (1, 4)))
    gate_weight = noise(key_list[1], (D, FF), D ** -0.5, 0.0625, ((0, 4), (1, 8)))
    up_weight = noise(key_list[2], (D, FF), D ** -0.5, 0.0625, ((0, 4), (1, 8)))
    down_weight = noise(key_list[3], (FF, D), FF ** -0.5, 0.03125, ((0, 8), (1, 4)))
    adapter_proj_in = noise(key_list[4], (NADAPT, 2 * R, D), D ** -0.5, 0.0625, ((0, 8), (2, 4)))
    adapter_lift_in = noise(key_list[5], (NADAPT, 2, R, FF), R ** -0.5, 1.5, ((0, 4), (3, 8)))
    adapter_proj_out = noise(key_list[6], (NADAPT, R, FF), FF ** -0.5, 0.03125, ((0, 4), (2, 8)))
    adapter_lift_out = noise(key_list[7], (NADAPT, R, D), R ** -0.5, 1.5, ((0, 8), (2, 4)))
    token_request = jnp.searchsorted(jnp.cumsum(uneven_parts(key_list[8], NREQ, TOKENS, 2 * TOK_DEV // REQ_DEV, 2)), jnp.arange(TOKENS), side="right").astype(jnp.int32)
    request_adapter = with_ends(skewed_ids(key_list[9], (NREQ,), NADAPT, 2), jax.random.fold_in(key_list[9], 3), 0, NADAPT - 1).astype(jnp.int32)
    adapter_slot = jax.random.permutation(key_list[10], NADAPT).astype(jnp.int32)
    return {"tokens": tokens, "gate_weight": gate_weight, "up_weight": up_weight, "down_weight": down_weight, "adapter_proj_in": adapter_proj_in, "adapter_lift_in": adapter_lift_in, "adapter_proj_out": adapter_proj_out, "adapter_lift_out": adapter_lift_out, "token_request": token_request, "request_adapter": request_adapter, "adapter_slot": adapter_slot}


def reference(tokens, gate_weight, up_weight, down_weight, adapter_proj_in, adapter_lift_in, adapter_proj_out, adapter_lift_out, token_request, request_adapter, adapter_slot):
    slot = adapter_slot[request_adapter[token_request]].astype(jnp.int32)

    def enter_one(pair):
        row_data, place = pair
        matrix = lax.dynamic_index_in_dim(adapter_proj_in, place, 0, keepdims=False).astype(jnp.float32)
        return jnp.dot(matrix, row_data.astype(jnp.float32))

    low_in = lax.map(enter_one, (tokens, slot)).astype(jnp.bfloat16)
    low_pairs = low_in.reshape(TOKENS, 2, R)

    def lift_one(pair):
        low_row, place = pair
        matrix = lax.dynamic_index_in_dim(adapter_lift_in, place, 0, keepdims=False).astype(jnp.float32)
        return jnp.einsum("cr,crf->cf", low_row.astype(jnp.float32), matrix)

    adapt_in = lax.map(lift_one, (low_pairs, slot))
    owner_in = slot // (NADAPT // N_TENSOR)
    width = D // N_TENSOR
    gate = jnp.zeros((TOKENS, FF), jnp.float32)
    up = jnp.zeros((TOKENS, FF), jnp.float32)
    for block in range(N_TENSOR):
        piece = tokens[:, block * width:(block + 1) * width]
        chosen = (owner_in == block).astype(jnp.float32)[:, None]
        gate_part = jnp.dot(piece, gate_weight[block * width:(block + 1) * width], preferred_element_type=jnp.float32) + chosen * adapt_in[:, 0]
        up_part = jnp.dot(piece, up_weight[block * width:(block + 1) * width], preferred_element_type=jnp.float32) + chosen * adapt_in[:, 1]
        gate = gate + lax.optimization_barrier(gate_part.astype(jnp.bfloat16)).astype(jnp.float32)
        up = up + lax.optimization_barrier(up_part.astype(jnp.bfloat16)).astype(jnp.float32)
    hidden = (jax.nn.silu(gate) * up).astype(jnp.bfloat16)

    def leave_one(pair):
        row_data, place = pair
        matrix = lax.dynamic_index_in_dim(adapter_proj_out, place, 0, keepdims=False).astype(jnp.float32)
        return jnp.dot(matrix, row_data.astype(jnp.float32))

    low_out = lax.map(leave_one, (hidden, slot)).astype(jnp.bfloat16)

    def back_one(pair):
        low_row, place = pair
        matrix = lax.dynamic_index_in_dim(adapter_lift_out, place, 0, keepdims=False).astype(jnp.float32)
        return jnp.dot(low_row.astype(jnp.float32), matrix)

    adapt_out = lax.map(back_one, (low_out, slot))
    owner_out = slot // (NADAPT // N_DP)
    span = FF // N_DP
    total = jnp.zeros((TOKENS, D), jnp.float32)
    for block in range(N_DP):
        chosen = (owner_out == block).astype(jnp.float32)[:, None]
        term = jnp.dot(hidden[:, block * span:(block + 1) * span], down_weight[block * span:(block + 1) * span], preferred_element_type=jnp.float32) + chosen * adapt_out
        total = total + lax.optimization_barrier(term.astype(jnp.bfloat16)).astype(jnp.float32)
    return total.astype(jnp.bfloat16)
```

```python
import functools

import jax
import jax.numpy as jnp
from jax import lax
from jax.experimental import pallas as pl
from jax.experimental.pallas import tpu as pltpu
from jax.sharding import PartitionSpec as P

CHUNKS = 4
F32 = jnp.float32
BF16 = jnp.bfloat16


def lookup(keys, table):
    hits = keys[:, None] == jnp.arange(table.shape[0], dtype=jnp.int32)[None, :]
    return jnp.sum(jnp.where(hits, table[None, :], 0), axis=1)


def owned(slot_of, first_slot, amount):
    places = first_slot + jnp.arange(amount, dtype=jnp.int32)
    return (slot_of[:, None] == places[None, :]).astype(jnp.bfloat16)


def general_device(
    tokens,
    gate_weight,
    up_weight,
    down_weight,
    adapter_proj_in,
    adapter_lift_in,
    adapter_proj_out,
    adapter_lift_out,
    token_request,
    request_adapter,
    adapter_slot,
):
    slot_of = lookup(lookup(token_request, request_adapter), adapter_slot)
    dp_index = lax.axis_index("dp")
    tensor_index = lax.axis_index("tensor")
    per_dp = adapter_proj_in.shape[0]
    per_tensor = adapter_lift_in.shape[0]
    rank = adapter_lift_out.shape[1]
    gathered = lax.all_gather(tokens, "dp", axis=0, tiled=True)
    total_rows = gathered.shape[0]
    mask_store_dp = owned(slot_of, dp_index * per_dp, per_dp)
    mask_store_tensor = owned(slot_of, tensor_index * per_tensor, per_tensor)
    projected = jnp.einsum(
        "td,srd->tsr", gathered, adapter_proj_in, preferred_element_type=jnp.float32
    )
    rank_part = jnp.sum(projected * mask_store_dp.astype(jnp.float32)[:, :, None], axis=1)
    rank_in = lax.psum(rank_part, ("dp", "tensor")).astype(jnp.bfloat16)
    rank_in = rank_in.reshape(total_rows, 2, rank)
    spread = rank_in[:, None, :, :] * mask_store_tensor[:, :, None, None]
    adapt_in = jnp.einsum(
        "tscr,scrf->tcf", spread, adapter_lift_in, preferred_element_type=jnp.float32
    )
    row_block = gathered
    gate_part = jnp.dot(row_block, gate_weight, preferred_element_type=jnp.float32)
    up_part = jnp.dot(row_block, up_weight, preferred_element_type=jnp.float32)
    extra = adapt_in
    shares = lax.psum_scatter(
        (jnp.stack([gate_part, up_part], axis=1) + extra).astype(jnp.bfloat16),
        "tensor",
        scatter_dimension=0,
        tiled=True,
    ).astype(jnp.float32)
    hidden = (jax.nn.silu(shares[:, 0]) * shares[:, 1]).astype(jnp.bfloat16)
    hidden_all = lax.all_gather(hidden, "tensor", axis=0, tiled=True)
    projected_out = jnp.einsum(
        "tf,srf->tsr", hidden_all, adapter_proj_out, preferred_element_type=jnp.float32
    )
    rank_part_out = jnp.sum(
        projected_out * mask_store_tensor.astype(jnp.float32)[:, :, None], axis=1
    )
    rank_out = lax.psum(rank_part_out, ("dp", "tensor")).astype(jnp.bfloat16)
    spread_out = rank_out[:, None, :] * mask_store_dp[:, :, None]
    adapt_out = jnp.einsum(
        "tsr,srd->td", spread_out, adapter_lift_out, preferred_element_type=jnp.float32
    )
    row_block = hidden_all
    extra = adapt_out
    return lax.psum_scatter(
        (jnp.dot(row_block, down_weight, preferred_element_type=jnp.float32) + extra).astype(
            jnp.bfloat16
        ),
        "dp",
        scatter_dimension=0,
        tiled=True,
    )


INWARD = [(0, 1), (3, 2)]
MIDDLE = [(1, 2), (2, 1)]
OUTWARD = [(1, 0), (2, 3)]


def masked_project(block, rows, slot_row, first):
    slots, rank, depth = block.shape
    full = lax.dot_general(
        block.reshape(slots * rank, depth), rows, (((1,), (1,)), ((), ())), preferred_element_type=F32
    ).reshape(slots, rank, rows.shape[0])
    ids = first + lax.broadcasted_iota(jnp.int32, full.shape, 0)
    return jnp.sum(jnp.where(ids == slot_row[None], full, 0.0), axis=0)


def spread_rows(rank_t, slot_col, slots):
    rank = rank_t.shape[0]
    width = slots * rank
    lane = lax.broadcasted_iota(jnp.int32, (rank, width), 1)
    row = lax.broadcasted_iota(jnp.int32, (rank, width), 0)
    copies = (lax.rem(lane, rank) == row).astype(F32).astype(BF16)
    tiled = lax.dot_general(
        rank_t.astype(F32).T.astype(BF16), copies, (((1,), (0,)), ((), ())), preferred_element_type=F32
    )
    owner = lax.div(lax.broadcasted_iota(jnp.int32, tiled.shape, 1), rank)
    return jnp.where(owner == slot_col, tiled, 0.0).astype(BF16)


def rank_in_kernel(slot_ref, rows_ref, proj_ref, out_ref):
    step = pl.program_id(0)
    part = masked_project(proj_ref[...], rows_ref[...], slot_ref[...], step * proj_ref.shape[0])

    @pl.when(step == 0)
    def _():
        out_ref[...] = part

    @pl.when(step > 0)
    def _():
        out_ref[...] += part


def rank_in_call(slot_row, rows, proj):
    slots, rank, depth = proj.shape
    total = rows.shape[0]
    group = 8
    return pl.pallas_call(
        rank_in_kernel,
        grid=(slots // group,),
        in_specs=[
            pl.BlockSpec((1, total), lambda s: (0, 0)),
            pl.BlockSpec((total, depth), lambda s: (0, 0)),
            pl.BlockSpec((group, rank, depth), lambda s: (s, 0, 0)),
        ],
        out_specs=pl.BlockSpec((rank, total), lambda s: (0, 0)),
        out_shape=jax.ShapeDtypeStruct((rank, total), F32),
        compiler_params=pltpu.CompilerParams(vmem_limit_bytes=32 << 20),
        cost_estimate=pl.CostEstimate(
            flops=2 * total * slots * rank * depth,
            bytes_accessed=2 * proj.size + 2 * rows.size,
            transcendentals=0,
        ),
        name="rank_in",
    )(slot_row, rows, proj)


def lift_kernel(side_ref, slot_ref, rank_ref, gate_ref, up_ref, lift_ref, near_ref, far_ref, total_ref):
    slots, _, rank, width = lift_ref.shape
    half = near_ref.shape[1]
    side = side_ref[0]
    for c, main_ref in ((0, gate_ref), (1, up_ref)):
        spread = spread_rows(rank_ref[c * rank:(c + 1) * rank, :], slot_ref[...], slots)
        matrix = lift_ref[:, c].reshape(slots * rank, width)
        total_ref[c] = main_ref[...] + jnp.dot(spread, matrix, preferred_element_type=F32)
        near_ref[c] = total_ref[c, pl.ds(pl.multiple_of(side * half, 16), half), :].astype(BF16)
        far_ref[c] = total_ref[c, pl.ds(pl.multiple_of((1 - side) * half, 16), half), :].astype(BF16)


def lift_call(chunk, side, slot_col, rank_t, gate_part, up_part, lift):
    slots, _, rank, wide = lift.shape
    width = wide // CHUNKS
    total = gate_part.shape[0]
    sub = 1
    cell = width // sub
    piece = jax.ShapeDtypeStruct((2, total // 2, width), BF16)
    return pl.pallas_call(
        lift_kernel,
        grid_spec=pltpu.PrefetchScalarGridSpec(
            num_scalar_prefetch=1,
            grid=(sub,),
            in_specs=[
                pl.BlockSpec((total, 1), lambda s, _: (0, 0)),
                pl.BlockSpec((2 * rank, total), lambda s, _: (0, 0)),
                pl.BlockSpec((total, cell), lambda s, _: (0, chunk * sub + s)),
                pl.BlockSpec((total, cell), lambda s, _: (0, chunk * sub + s)),
                pl.BlockSpec((slots, 2, rank, cell), lambda s, _: (0, 0, 0, chunk * sub + s)),
            ],
            out_specs=[pl.BlockSpec((2, total // 2, cell), lambda s, _: (0, 0, s))] * 2,
            scratch_shapes=[pltpu.VMEM((2, total, cell), F32)],
        ),
        out_shape=[piece, piece],
        compiler_params=pltpu.CompilerParams(vmem_limit_bytes=40 << 20),
        cost_estimate=pl.CostEstimate(
            flops=4 * total * slots * rank * width,
            bytes_accessed=4 * slots * rank * width + 16 * total * width,
            transcendentals=0,
        ),
        name="lift",
    )(side, slot_col, rank_t, gate_part, up_part, lift)


def down_kernel(first, side_ref, slot_ref, near_ref, far_ref, down_ref, proj_ref, *rest):
    if first:
        sum_ref, rank_ref, hidden_ref = rest
    else:
        sum_in_ref, rank_in_ref, sum_ref, rank_ref, hidden_ref = rest
    step = pl.program_id(0)
    half = near_ref.shape[0]
    side = side_ref[0]

    @pl.when(step == 0)
    def _():
        hidden_ref[pl.ds(pl.multiple_of(side * half, 16), half), :] = near_ref[...]
        hidden_ref[pl.ds(pl.multiple_of((1 - side) * half, 16), half), :] = far_ref[...]
        rank_ref[...] = jnp.zeros_like(rank_ref) if first else rank_in_ref[...]

    hidden = hidden_ref[...]
    product = jnp.dot(hidden, down_ref[...], preferred_element_type=F32)
    sum_ref[...] = product if first else product + sum_in_ref[...]
    rank_ref[...] += masked_project(proj_ref[...], hidden, slot_ref[...], step * proj_ref.shape[0])


def down_call(chunk, side, slot_row, near, far, down, proj, carried):
    slots, rank, wide = proj.shape
    half, width = near.shape
    total = 2 * half
    out = down.shape[1]
    steps = 4
    cell = out // steps
    first = carried is None
    in_specs = [
        pl.BlockSpec((1, total), lambda s, _: (0, 0)),
        pl.BlockSpec((half, width), lambda s, _: (0, 0)),
        pl.BlockSpec((half, width), lambda s, _: (0, 0)),
        pl.BlockSpec((width, cell), lambda s, _: (chunk, s)),
        pl.BlockSpec((slots // steps, rank, width), lambda s, _: (s, 0, chunk)),
    ]
    out_specs = [
        pl.BlockSpec((total, cell), lambda s, _: (0, s)),
        pl.BlockSpec((rank, total), lambda s, _: (0, 0)),
    ]
    if not first:
        in_specs += out_specs
    return pl.pallas_call(
        functools.partial(down_kernel, first),
        grid_spec=pltpu.PrefetchScalarGridSpec(
            num_scalar_prefetch=1,
            grid=(steps,),
            in_specs=in_specs,
            out_specs=out_specs,
            scratch_shapes=[pltpu.VMEM((total, width), BF16)],
        ),
        out_shape=[
            jax.ShapeDtypeStruct((total, out), F32),
            jax.ShapeDtypeStruct((rank, total), F32),
        ],
        compiler_params=pltpu.CompilerParams(vmem_limit_bytes=32 << 20),
        cost_estimate=pl.CostEstimate(
            flops=2 * total * width * (out + slots * rank),
            bytes_accessed=2 * width * (out + slots * rank) + 8 * total * out,
            transcendentals=0,
        ),
        name="down",
    )(side, slot_row, near, far, down, proj, *(() if first else carried))


def last_kernel(slot_ref, rank_ref, sum_ref, lift_ref, out_ref):
    slots, rank, width = lift_ref.shape
    spread = spread_rows(rank_ref[...], slot_ref[...], slots)
    extra = jnp.dot(spread, lift_ref[...].reshape(slots * rank, width), preferred_element_type=F32)
    out_ref[...] = (sum_ref[...] + extra).astype(BF16)


def last_call(slot_col, rank_t, sums, lift):
    slots, rank, out = lift.shape
    total = sums.shape[0]
    cell = out // 4
    return pl.pallas_call(
        last_kernel,
        grid=(4,),
        in_specs=[
            pl.BlockSpec((total, 1), lambda s: (0, 0)),
            pl.BlockSpec((rank, total), lambda s: (0, 0)),
            pl.BlockSpec((total, cell), lambda s: (0, s)),
            pl.BlockSpec((slots, rank, cell), lambda s: (0, 0, s)),
        ],
        out_specs=pl.BlockSpec((total, cell), lambda s: (0, s)),
        out_shape=jax.ShapeDtypeStruct((total, out), BF16),
        compiler_params=pltpu.CompilerParams(vmem_limit_bytes=32 << 20),
        cost_estimate=pl.CostEstimate(
            flops=2 * total * slots * rank * out,
            bytes_accessed=2 * slots * rank * out + 6 * total * out,
            transcendentals=0,
        ),
        name="last",
    )(slot_col, rank_t, sums, lift)


def swap(value, axis, size, mask):
    return lax.ppermute(value, axis, [(i, i ^ mask) for i in range(size)])


def sum_everywhere(value):
    value = value + swap(value, "dp", 8, 1)
    value = value + swap(value, "dp", 8, 2) + swap(value, "dp", 8, 4) + swap(value, "dp", 8, 6)
    return value + swap(value, "tensor", 4, 1) + swap(value, "tensor", 4, 2) + swap(value, "tensor", 4, 3)


def widen_sum(one, two):
    return (one.astype(F32) + two.astype(F32)).astype(BF16)


def scatter_dp(rows):
    total, width = rows.shape
    me = lax.axis_index("dp")
    core = me % 2
    blocks = rows.reshape(4, 2, total // 8, width)
    mine = lax.dynamic_index_in_dim(blocks, core, 1, keepdims=False)
    other = lax.dynamic_index_in_dim(blocks, 1 - core, 1, keepdims=False)
    both = widen_sum(mine, swap(other, "dp", 8, 1))
    chip = me // 2
    kept = lax.dynamic_index_in_dim(both, chip, 0, keepdims=False).astype(F32)
    for mask in (3, 1, 2):
        sent = lax.dynamic_index_in_dim(both, chip ^ mask, 0, keepdims=False)
        kept = kept + swap(sent, "dp", 8, 2 * mask).astype(F32)
    return kept.astype(BF16)


def line_device(
    tokens,
    gate_weight,
    up_weight,
    down_weight,
    adapter_proj_in,
    adapter_lift_in,
    adapter_proj_out,
    adapter_lift_out,
    token_request,
    request_adapter,
    adapter_slot,
):
    slot_of = lookup(lookup(token_request, request_adapter), adapter_slot)
    dp_index = lax.axis_index("dp")
    tensor_index = lax.axis_index("tensor")
    side = (tensor_index // 2).astype(jnp.int32).reshape(1)
    is_end = (tensor_index == 0) | (tensor_index == 3)
    slot_dp = slot_of - dp_index * adapter_proj_in.shape[0]
    slot_tensor = slot_of - tensor_index * adapter_lift_in.shape[0]
    gathered = lax.all_gather(tokens, "dp", axis=0, tiled=True)
    rank_part = rank_in_call(slot_dp[None, :], gathered, adapter_proj_in)
    gate_part = jnp.dot(gathered, gate_weight, preferred_element_type=F32)
    up_part = jnp.dot(gathered, up_weight, preferred_element_type=F32)
    rank_in = sum_everywhere(rank_part).astype(BF16)
    carried = None
    for chunk in range(CHUNKS):
        near, far = lift_call(
            chunk, side, slot_tensor[:, None], rank_in, gate_part, up_part, adapter_lift_in
        )
        arrived = lax.ppermute(far, "tensor", INWARD)
        arrived = lax.ppermute(widen_sum(far, arrived), "tensor", MIDDLE)
        near = widen_sum(near, arrived)
        arrived = lax.ppermute(near, "tensor", OUTWARD)
        gate = near[0].astype(F32) + arrived[0].astype(F32)
        up = near[1].astype(F32) + arrived[1].astype(F32)
        hidden = (jax.nn.silu(gate) * up).astype(BF16)
        arrived = lax.ppermute(hidden, "tensor", INWARD)
        hidden_near = jnp.where(is_end, hidden, arrived)
        crossed = lax.ppermute(arrived, "tensor", MIDDLE)
        returned = lax.ppermute(crossed, "tensor", OUTWARD)
        hidden_far = jnp.where(is_end, returned, crossed)
        carried = down_call(
            chunk, side, slot_tensor[None, :], hidden_near, hidden_far, down_weight, adapter_proj_out, carried
        )
    sums, rank_part_out = carried
    rank_out = sum_everywhere(rank_part_out).astype(BF16)
    return scatter_dp(last_call(slot_dp[:, None], rank_out, sums, adapter_lift_out))


def solution(mesh):
    on_line = mesh.shape["tensor"] == 4 and mesh.shape["dp"] == 8
    placed = (
        P("dp", "tensor"),
        P("tensor", "dp"),
        P("tensor", "dp"),
        P("dp", "tensor"),
        P("dp", None, "tensor"),
        P("tensor", None, None, "dp"),
        P("tensor", None, "dp"),
        P("dp", None, "tensor"),
        P(),
        P(),
        P(),
    )
    return jax.shard_map(
        line_device if on_line else general_device, mesh=mesh, in_specs=placed, out_specs=P("dp", "tensor"), check_vma=False
    )
```

```python
import functools

import jax
import jax.numpy as jnp
from jax import lax
from jax.experimental import pallas as pl
from jax.experimental.pallas import tpu as pltpu
from jax.sharding import PartitionSpec as P

CELL = 256
DOWN_CELL = 512
CHUNKS = (4, 5, 5)
VMEM_LIMIT = 40 << 20
LIGHT = pl.CostEstimate(flops=1024, bytes_accessed=1024, transcendentals=0)
F32 = jnp.float32
BF16 = jnp.bfloat16


def lookup(keys, table):
    hits = keys[:, None] == jnp.arange(table.shape[0], dtype=jnp.int32)[None, :]
    return jnp.sum(jnp.where(hits, table[None, :], 0), axis=1)


def owned(slot_of, first_slot, amount):
    places = first_slot + jnp.arange(amount, dtype=jnp.int32)
    return (slot_of[:, None] == places[None, :]).astype(jnp.bfloat16)


def general_device(
    tokens,
    gate_weight,
    up_weight,
    down_weight,
    adapter_proj_in,
    adapter_lift_in,
    adapter_proj_out,
    adapter_lift_out,
    token_request,
    request_adapter,
    adapter_slot,
):
    slot_of = lookup(lookup(token_request, request_adapter), adapter_slot)
    dp_index = lax.axis_index("dp")
    tensor_index = lax.axis_index("tensor")
    per_dp = adapter_proj_in.shape[0]
    per_tensor = adapter_lift_in.shape[0]
    rank = adapter_lift_out.shape[1]
    gathered = lax.all_gather(tokens, "dp", axis=0, tiled=True)
    total_rows = gathered.shape[0]
    mask_store_dp = owned(slot_of, dp_index * per_dp, per_dp)
    mask_store_tensor = owned(slot_of, tensor_index * per_tensor, per_tensor)
    projected = jnp.einsum(
        "td,srd->tsr", gathered, adapter_proj_in, preferred_element_type=jnp.float32
    )
    rank_part = jnp.sum(projected * mask_store_dp.astype(jnp.float32)[:, :, None], axis=1)
    rank_in = lax.psum(rank_part, ("dp", "tensor")).astype(jnp.bfloat16)
    rank_in = rank_in.reshape(total_rows, 2, rank)
    spread = rank_in[:, None, :, :] * mask_store_tensor[:, :, None, None]
    adapt_in = jnp.einsum(
        "tscr,scrf->tcf", spread, adapter_lift_in, preferred_element_type=jnp.float32
    )
    row_block = gathered
    gate_part = jnp.dot(row_block, gate_weight, preferred_element_type=jnp.float32)
    up_part = jnp.dot(row_block, up_weight, preferred_element_type=jnp.float32)
    extra = adapt_in
    shares = lax.psum_scatter(
        (jnp.stack([gate_part, up_part], axis=1) + extra).astype(jnp.bfloat16),
        "tensor",
        scatter_dimension=0,
        tiled=True,
    ).astype(jnp.float32)
    hidden = (jax.nn.silu(shares[:, 0]) * shares[:, 1]).astype(jnp.bfloat16)
    hidden_all = lax.all_gather(hidden, "tensor", axis=0, tiled=True)
    projected_out = jnp.einsum(
        "tf,srf->tsr", hidden_all, adapter_proj_out, preferred_element_type=jnp.float32
    )
    rank_part_out = jnp.sum(
        projected_out * mask_store_tensor.astype(jnp.float32)[:, :, None], axis=1
    )
    rank_out = lax.psum(rank_part_out, ("dp", "tensor")).astype(jnp.bfloat16)
    spread_out = rank_out[:, None, :] * mask_store_dp[:, :, None]
    adapt_out = jnp.einsum(
        "tsr,srd->td", spread_out, adapter_lift_out, preferred_element_type=jnp.float32
    )
    row_block = hidden_all
    extra = adapt_out
    return lax.psum_scatter(
        (jnp.dot(row_block, down_weight, preferred_element_type=jnp.float32) + extra).astype(
            jnp.bfloat16
        ),
        "dp",
        scatter_dimension=0,
        tiled=True,
    )


OUTER = [(0, 1), (1, 0), (2, 3), (3, 2)]
MIDDLE = [(1, 2), (2, 1)]


def masked_project(block, rows, slot_row, first):
    slots, rank, depth = block.shape
    full = lax.dot_general(
        block.reshape(slots * rank, depth), rows, (((1,), (1,)), ((), ())), preferred_element_type=F32
    ).reshape(slots, rank, rows.shape[0])
    ids = first + lax.broadcasted_iota(jnp.int32, full.shape, 0)
    return jnp.sum(jnp.where(ids == slot_row[None], full, 0.0), axis=0)


def spread_rows(rank_t, slot_col, slots):
    rank = rank_t.shape[0]
    width = slots * rank
    lane = lax.broadcasted_iota(jnp.int32, (rank, width), 1)
    row = lax.broadcasted_iota(jnp.int32, (rank, width), 0)
    copies = (lax.rem(lane, rank) == row).astype(F32).astype(BF16)
    tiled = lax.dot_general(
        rank_t.astype(F32).T.astype(BF16), copies, (((1,), (0,)), ((), ())), preferred_element_type=F32
    )
    owner = lax.div(lax.broadcasted_iota(jnp.int32, tiled.shape, 1), rank)
    return jnp.where(owner == slot_col, tiled, 0.0).astype(BF16)


def rank_in_kernel(slot_ref, rows_ref, proj_ref, out_ref):
    step = pl.program_id(0)
    part = masked_project(proj_ref[...], rows_ref[...], slot_ref[...], step * proj_ref.shape[0])

    @pl.when(step == 0)
    def _():
        out_ref[...] = part

    @pl.when(step > 0)
    def _():
        out_ref[...] += part


def rank_in_call(slot_row, rows, proj):
    slots, rank, depth = proj.shape
    total = rows.shape[0]
    group = 8
    return pl.pallas_call(
        rank_in_kernel,
        grid=(slots // group,),
        in_specs=[
            pl.BlockSpec((1, total), lambda s: (0, 0)),
            pl.BlockSpec((total, depth), lambda s: (0, 0)),
            pl.BlockSpec((group, rank, depth), lambda s: (s, 0, 0)),
        ],
        out_specs=pl.BlockSpec((rank, total), lambda s: (0, 0)),
        out_shape=jax.ShapeDtypeStruct((rank, total), F32),
        compiler_params=pltpu.CompilerParams(vmem_limit_bytes=VMEM_LIMIT),
        cost_estimate=LIGHT,
        name="rank_in",
    )(slot_row, rows, proj)


def half_rows(side, which, half):
    start = side * half if which == 0 else (1 - side) * half
    return pl.ds(pl.multiple_of(start, 16), half)


def main_kernel(rows_ref, gate_ref, up_ref, out_ref):
    for c, main_ref in ((0, gate_ref), (1, up_ref)):
        out_ref[c] = jnp.dot(rows_ref[...], main_ref[...], preferred_element_type=F32)


def main_call(first, cells, rows, gate_weight, up_weight):
    total, depth = rows.shape
    weight = pl.BlockSpec((depth, CELL), lambda s: (0, first + s))
    return pl.pallas_call(
        main_kernel,
        grid=(cells,),
        in_specs=[pl.BlockSpec((total, depth), lambda s: (0, 0)), weight, weight],
        out_specs=pl.BlockSpec((2, total, CELL), lambda s: (0, 0, s)),
        out_shape=jax.ShapeDtypeStruct((2, total, cells * CELL), F32),
        compiler_params=pltpu.CompilerParams(vmem_limit_bytes=VMEM_LIMIT),
        cost_estimate=LIGHT,
        name="main",
    )(rows, gate_weight, up_weight)


def halves_out(total_ref, side, near_ref, far_ref):
    half = near_ref.shape[1]
    for c in range(2):
        near_ref[c] = total_ref[c, half_rows(side, 0, half), :].astype(BF16)
        far_ref[c] = total_ref[c, half_rows(side, 1, half), :].astype(BF16)


def lift_part(lift_ref, spread_ref, c):
    slots, _, rank, width = lift_ref.shape
    return jnp.dot(spread_ref[c], lift_ref[:, c].reshape(slots * rank, width), preferred_element_type=F32)


def first_kernel(side_ref, slot_ref, rank_ref, lift_ref, *rest):
    *mains, near_ref, far_ref, spread_ref, total_ref = rest
    slots, _, rank, _ = lift_ref.shape
    step = pl.program_id(0)

    @pl.when(step == 0)
    def _():
        for c in range(2):
            spread_ref[c] = spread_rows(rank_ref[c * rank:(c + 1) * rank, :], slot_ref[...], slots)

    for c in range(2):
        total_ref[c] = mains[0][c] + lift_part(lift_ref, spread_ref, c)
    halves_out(total_ref, side_ref[0], near_ref, far_ref)


def first_call(cells, side, slot_col, rank_t, main, lift):
    slots, _, rank, _ = lift.shape
    total = main.shape[1]
    half = total // 2
    piece = jax.ShapeDtypeStruct((2, half, cells * CELL), BF16)
    piece_spec = pl.BlockSpec((2, half, CELL), lambda s, _: (0, 0, s))
    return pl.pallas_call(
        first_kernel,
        grid_spec=pltpu.PrefetchScalarGridSpec(
            num_scalar_prefetch=1,
            grid=(cells,),
            in_specs=[
                pl.BlockSpec((total, 1), lambda s, _: (0, 0)),
                pl.BlockSpec((2 * rank, total), lambda s, _: (0, 0)),
                pl.BlockSpec((slots, 2, rank, CELL), lambda s, _: (0, 0, 0, s)),
                pl.BlockSpec((2, total, CELL), lambda s, _: (0, 0, s)),
            ],
            out_specs=[piece_spec, piece_spec, pl.BlockSpec((2, total, slots * rank), lambda s, _: (0, 0, 0))],
            scratch_shapes=[pltpu.VMEM((2, total, CELL), F32)],
        ),
        out_shape=[piece, piece, jax.ShapeDtypeStruct((2, total, slots * rank), BF16)],
        compiler_params=pltpu.CompilerParams(vmem_limit_bytes=VMEM_LIMIT),
        cost_estimate=LIGHT,
        name="first",
    )(side, slot_col, rank_t, lift, main)


def into_kernel(side_ref, rows_ref, gate_ref, up_ref, lift_ref, spread_ref, near_ref, far_ref, total_ref):
    for c, main_ref in ((0, gate_ref), (1, up_ref)):
        total_ref[c] = jnp.dot(rows_ref[...], main_ref[...], preferred_element_type=F32) + lift_part(
            lift_ref, spread_ref, c
        )
    halves_out(total_ref, side_ref[0], near_ref, far_ref)


def into_call(first, cells, side, spread, rows, gate_weight, up_weight, lift):
    slots, _, rank, _ = lift.shape
    total, depth = rows.shape
    weight = pl.BlockSpec((depth, CELL), lambda s, _: (0, first + s))
    return pl.pallas_call(
        into_kernel,
        grid_spec=pltpu.PrefetchScalarGridSpec(
            num_scalar_prefetch=1,
            grid=(cells,),
            in_specs=[
                pl.BlockSpec((total, depth), lambda s, _: (0, 0)),
                weight,
                weight,
                pl.BlockSpec((slots, 2, rank, CELL), lambda s, _: (0, 0, 0, first + s)),
                pl.BlockSpec(spread.shape, lambda s, _: (0, 0, 0)),
            ],
            out_specs=[pl.BlockSpec((2, total // 2, CELL), lambda s, _: (0, 0, s))] * 2,
            scratch_shapes=[pltpu.VMEM((2, total, CELL), F32)],
        ),
        out_shape=[jax.ShapeDtypeStruct((2, total // 2, cells * CELL), BF16)] * 2,
        compiler_params=pltpu.CompilerParams(vmem_limit_bytes=VMEM_LIMIT),
        cost_estimate=LIGHT,
        name="into",
    )(side, rows, gate_weight, up_weight, lift, spread)


def project_kernel(pieces, side_ref, slot_ref, proj_ref, *rest):
    parts, rest = rest[:2 * pieces], rest[2 * pieces:]
    out_ref, hidden_ref = rest[-2:]
    step = pl.program_id(0)
    side = side_ref[0]

    @pl.when(step == 0)
    def _():
        at = 0
        for piece in range(pieces):
            for which in range(2):
                part_ref = parts[2 * piece + which]
                half, width = part_ref.shape
                for cell in range(width // CELL):
                    hidden_ref[at + cell, half_rows(side, which, half), :] = part_ref[:, cell * CELL:(cell + 1) * CELL]
            at += width // CELL
        out_ref[...] = rest[0][...] if len(rest) == 3 else jnp.zeros(out_ref.shape, F32)

    out_ref[...] += masked_project(proj_ref[...], hidden_ref[step], slot_ref[...], 0)


def project_call(first, side, slot_row, parts, proj, carried):
    slots, rank, _ = proj.shape
    half = parts[0].shape[0]
    cells = sum(part.shape[1] for part in parts) // 2 // CELL
    extra = () if carried is None else (carried,)
    fixed = lambda shape: pl.BlockSpec(shape, lambda s, _: (0, 0))
    return pl.pallas_call(
        functools.partial(project_kernel, len(parts) // 2),
        grid_spec=pltpu.PrefetchScalarGridSpec(
            num_scalar_prefetch=1,
            grid=(cells,),
            in_specs=[
                fixed((1, 2 * half)),
                pl.BlockSpec((slots, rank, CELL), lambda s, _: (0, 0, first + s)),
            ]
            + [fixed(part.shape) for part in parts]
            + [fixed(one.shape) for one in extra],
            out_specs=fixed((rank, 2 * half)),
            scratch_shapes=[pltpu.VMEM((cells, 2 * half, CELL), BF16)],
        ),
        out_shape=jax.ShapeDtypeStruct((rank, 2 * half), F32),
        compiler_params=pltpu.CompilerParams(vmem_limit_bytes=VMEM_LIMIT),
        cost_estimate=LIGHT,
        name="project",
    )(side, slot_row, proj, *parts, *extra)


def down_kernel(pieces, cells, side_ref, *rest):
    downs, parts, rest = rest[:cells], rest[cells:cells + 2 * pieces], rest[cells + 2 * pieces:]
    out_ref, hidden_ref = rest[-2:]
    side = side_ref[0]

    @pl.when(pl.program_id(0) == 0)
    def _():
        at = 0
        for piece in range(pieces):
            for which in range(2):
                part_ref = parts[2 * piece + which]
                half, width = part_ref.shape
                hidden_ref[half_rows(side, which, half), at:at + width] = part_ref[...]
            at += width

    product = rest[0][...] if len(rest) == 3 else 0.0
    for cell in range(cells):
        columns = hidden_ref[:, cell * CELL:(cell + 1) * CELL]
        product += jnp.dot(columns, downs[cell][...], preferred_element_type=F32)
    out_ref[...] = product


def down_call(first, side, parts, down, carried):
    half = parts[0].shape[0]
    depth = sum(part.shape[1] for part in parts) // 2
    cells = depth // CELL
    out = down.shape[1]
    extra = () if carried is None else (carried,)
    wide = pl.BlockSpec((2 * half, DOWN_CELL), lambda s, _: (0, s))
    return pl.pallas_call(
        functools.partial(down_kernel, len(parts) // 2, cells),
        grid_spec=pltpu.PrefetchScalarGridSpec(
            num_scalar_prefetch=1,
            grid=(out // DOWN_CELL,),
            in_specs=[
                pl.BlockSpec((CELL, DOWN_CELL), lambda s, _, cell=cell: (first + cell, s)) for cell in range(cells)
            ]
            + [pl.BlockSpec(part.shape, lambda s, _: (0, 0)) for part in parts]
            + [wide for _ in extra],
            out_specs=wide,
            scratch_shapes=[pltpu.VMEM((2 * half, depth), BF16)],
        ),
        out_shape=jax.ShapeDtypeStruct((2 * half, out), F32),
        compiler_params=pltpu.CompilerParams(vmem_limit_bytes=VMEM_LIMIT),
        cost_estimate=LIGHT,
        name="down",
    )(side, *(down,) * cells, *parts, *extra)


def last_kernel(slot_ref, rank_ref, sum_ref, lift_ref, out_ref, spread_ref):
    slots, rank, width = lift_ref.shape

    @pl.when(pl.program_id(0) == 0)
    def _():
        spread_ref[...] = spread_rows(rank_ref[...], slot_ref[...], slots)

    extra = jnp.dot(spread_ref[...], lift_ref[...].reshape(slots * rank, width), preferred_element_type=F32)
    out_ref[...] = (sum_ref[...] + extra).astype(BF16)


def last_call(slot_col, rank_t, sums, lift):
    slots, rank, out = lift.shape
    total = sums.shape[0]
    return pl.pallas_call(
        last_kernel,
        grid=(out // DOWN_CELL,),
        in_specs=[
            pl.BlockSpec((total, 1), lambda s: (0, 0)),
            pl.BlockSpec((rank, total), lambda s: (0, 0)),
            pl.BlockSpec((total, DOWN_CELL), lambda s: (0, s)),
            pl.BlockSpec((slots, rank, DOWN_CELL), lambda s: (0, 0, s)),
        ],
        out_specs=pl.BlockSpec((total, DOWN_CELL), lambda s: (0, s)),
        out_shape=jax.ShapeDtypeStruct((total, out), BF16),
        scratch_shapes=[pltpu.VMEM((total, slots * rank), BF16)],
        compiler_params=pltpu.CompilerParams(vmem_limit_bytes=VMEM_LIMIT),
        cost_estimate=LIGHT,
        name="last",
    )(slot_col, rank_t, sums, lift)


def after(value, *behind):
    return lax.optimization_barrier((value, *behind))[0]


def swap(value, axis, size, mask):
    return lax.ppermute(value, axis, [(i, i ^ mask) for i in range(size)])


def sum_everywhere(value, beside=()):
    made = []
    for stage, (axis, size, mask) in enumerate(
        (("dp", 8, 1), ("dp", 8, 2), ("dp", 8, 4), ("tensor", 4, 1), ("tensor", 4, 2))
    ):
        other = swap(value, axis, size, mask)
        for when, work in beside:
            if when == stage:
                made.append(work(value, *made[-1:]))
                other, made[-1] = lax.optimization_barrier((other, made[-1]))
        value = value + other
    return value, made


def scatter_dp(rows):
    total, width = rows.shape
    me = lax.axis_index("dp")
    core = me & 1
    blocks = rows.reshape(4, 2, total // 8, width)
    mine = lax.dynamic_index_in_dim(blocks, core, 1, keepdims=False)
    other = lax.dynamic_index_in_dim(blocks, 1 - core, 1, keepdims=False)
    both = (mine.astype(F32) + swap(other, "dp", 8, 1).astype(F32)).astype(BF16)
    chip = me >> 1
    kept = lax.dynamic_index_in_dim(both, chip, 0, keepdims=False).astype(F32)
    for mask in (3, 1, 2):
        sent = lax.dynamic_index_in_dim(both, chip ^ mask, 0, keepdims=False)
        kept = kept + swap(sent, "dp", 8, 2 * mask).astype(F32)
    return kept.astype(BF16)


def line_device(
    tokens,
    gate_weight,
    up_weight,
    down_weight,
    adapter_proj_in,
    adapter_lift_in,
    adapter_proj_out,
    adapter_lift_out,
    token_request,
    request_adapter,
    adapter_slot,
):
    slot_of = lookup(lookup(token_request, request_adapter), adapter_slot)
    dp_index = lax.axis_index("dp")
    tensor_index = lax.axis_index("tensor")
    side = (tensor_index >> 1).astype(jnp.int32).reshape(1)
    is_end = (tensor_index == 0) | (tensor_index == 3)
    slot_dp = slot_of - dp_index * adapter_proj_in.shape[0]
    slot_tensor = slot_of - tensor_index * adapter_lift_in.shape[0]
    gathered = lax.all_gather(tokens, "dp", axis=0, tiled=True)
    rank_part = rank_in_call(slot_dp[None, :], gathered, adapter_proj_in)
    rank_in, mains = sum_everywhere(
        rank_part,
        [
            (1, lambda tie: main_call(0, CHUNKS[0], after(gathered, tie), gate_weight, up_weight)),
        ],
    )
    rank_in = rank_in.astype(BF16)
    slot_row = slot_tensor[None, :]
    slot_col = slot_tensor[:, None]
    chunks = len(CHUNKS)
    starts = [sum(CHUNKS[:c]) for c in range(chunks)]
    near, far, hop, hidden_near, hidden_far = ({} for _ in range(5))

    def operand(c, stage):
        if stage == 0:
            return far[c]
        if stage == 1:
            return (far[c].astype(F32) + hop[c].astype(F32)).astype(BF16)
        if stage == 2:
            return (near[c].astype(F32) + hop[c].astype(F32)).astype(BF16)
        if stage == 3:
            both = near[c].astype(F32) + hop[c].astype(F32)
            hidden_near[c] = (jax.nn.silu(both[0]) * both[1]).astype(BF16)[None]
            return hidden_near[c]
        if stage == 4:
            hidden_near[c] = jnp.where(is_end, hidden_near[c], hop[c])
            return hop[c]
        hidden_far[c] = hop[c]
        return hop[c]

    def pair(c):
        return [hidden_near[c][0], jnp.where(is_end, hop[c], hidden_far[c])[0]]

    def padded(value, shape):
        return jnp.pad(value, [(0, b - a) for a, b in zip(value.shape, shape)])

    near[0], far[0], spread = first_call(CHUNKS[0], side, slot_col, rank_in, mains[0], adapter_lift_in)
    sums, ranks = None, None
    for slot in range(chunks + 5):
        live = [(slot - stage, stage) for stage in range(6) if 0 <= slot - stage < chunks]
        values = {stage % 3: operand(c, stage) for c, stage in live}
        if 0 in values and 2 in values:
            shape = tuple(max(a, b) for a, b in zip(values[0].shape, values[2].shape))
            outer = jnp.where(is_end, padded(values[0], shape), padded(values[2], shape))
        else:
            outer = values.get(0, values.get(2))
        sent = [value for value in (outer, values.get(1)) if value is not None]
        sent = list(lax.optimization_barrier(tuple(sent)))
        arrived = {}
        if outer is not None:
            arrived[0] = lax.ppermute(sent[0], "tensor", OUTER)
        if 1 in values:
            arrived[1] = lax.ppermute(sent[-1], "tensor", MIDDLE)
        made = ()
        if slot + 1 < chunks:
            made = into_call(
                starts[slot + 1], CHUNKS[slot + 1], after(side, *sent), spread, gathered, gate_weight, up_weight, adapter_lift_in
            )
        done = slot - 6
        if done == 0:
            early = pair(0)
            ranks = project_call(starts[0], after(side, *sent), slot_row, early, adapter_proj_out, None)
            sums = down_call(starts[0], after(side, ranks), early, down_weight, None)
            made = (ranks, sums)
        elif done > 0:
            ranks = project_call(starts[done], after(side, *sent), slot_row, pair(done), adapter_proj_out, ranks)
            made = (ranks,)
        *came, = lax.optimization_barrier((*arrived.values(), *made))
        arrived = dict(zip(arrived, came))
        made = came[len(arrived):]
        if slot + 1 < chunks:
            near[slot + 1], far[slot + 1] = made
        elif done == 0:
            ranks, sums = made
        elif done > 0:
            (ranks,) = made
        for c, stage in live:
            value = arrived[stage % 3 % 2]
            units, width = (2, 1)[stage // 3], CHUNKS[c] * CELL
            hop[c] = value[:units, :, :width]
    ranks = project_call(starts[chunks - 1], side, slot_row, pair(chunks - 1), adapter_proj_out, ranks)
    rank_out, made = sum_everywhere(
        ranks,
        [
            (1, lambda tie: down_call(starts[1], after(side, tie), pair(1), down_weight, sums)),
            (3, lambda tie, before: down_call(starts[2], after(side, tie), pair(2), down_weight, before)),
        ],
    )
    return scatter_dp(last_call(slot_dp[:, None], rank_out.astype(BF16), made[-1], adapter_lift_out))


def solution(mesh):
    on_line = mesh.shape["tensor"] == 4 and mesh.shape["dp"] == 8
    placed = (
        P("dp", "tensor"),
        P("tensor", "dp"),
        P("tensor", "dp"),
        P("dp", "tensor"),
        P("dp", None, "tensor"),
        P("tensor", None, None, "dp"),
        P("tensor", None, "dp"),
        P("dp", None, "tensor"),
        P(),
        P(),
        P(),
    )
    return jax.shard_map(
        line_device if on_line else general_device, mesh=mesh, in_specs=placed, out_specs=P("dp", "tensor"), check_vma=False
    )
```

```python
import functools

import jax
import jax.numpy as jnp
from jax import lax
from jax.experimental import pallas as pl
from jax.experimental.pallas import tpu as pltpu
from jax.sharding import PartitionSpec as P

CELL = 256
CHUNKS = (4, 5, 5)
VMEM_LIMIT = 40 << 20
LIGHT = pl.CostEstimate(flops=1024, bytes_accessed=1024, transcendentals=0)
F32 = jnp.float32
BF16 = jnp.bfloat16


def lookup(keys, table):
    hits = keys[:, None] == jnp.arange(table.shape[0], dtype=jnp.int32)[None, :]
    return jnp.sum(jnp.where(hits, table[None, :], 0), axis=1)


def owned(slot_of, first_slot, amount):
    places = first_slot + jnp.arange(amount, dtype=jnp.int32)
    return (slot_of[:, None] == places[None, :]).astype(jnp.bfloat16)


def general_device(
    tokens,
    gate_weight,
    up_weight,
    down_weight,
    adapter_proj_in,
    adapter_lift_in,
    adapter_proj_out,
    adapter_lift_out,
    token_request,
    request_adapter,
    adapter_slot,
):
    slot_of = lookup(lookup(token_request, request_adapter), adapter_slot)
    dp_index = lax.axis_index("dp")
    tensor_index = lax.axis_index("tensor")
    per_dp = adapter_proj_in.shape[0]
    per_tensor = adapter_lift_in.shape[0]
    rank = adapter_lift_out.shape[1]
    gathered = lax.all_gather(tokens, "dp", axis=0, tiled=True)
    total_rows = gathered.shape[0]
    mask_store_dp = owned(slot_of, dp_index * per_dp, per_dp)
    mask_store_tensor = owned(slot_of, tensor_index * per_tensor, per_tensor)
    projected = jnp.einsum(
        "td,srd->tsr", gathered, adapter_proj_in, preferred_element_type=jnp.float32
    )
    rank_part = jnp.sum(projected * mask_store_dp.astype(jnp.float32)[:, :, None], axis=1)
    rank_in = lax.psum(rank_part, ("dp", "tensor")).astype(jnp.bfloat16)
    rank_in = rank_in.reshape(total_rows, 2, rank)
    spread = rank_in[:, None, :, :] * mask_store_tensor[:, :, None, None]
    adapt_in = jnp.einsum(
        "tscr,scrf->tcf", spread, adapter_lift_in, preferred_element_type=jnp.float32
    )
    row_block = gathered
    gate_part = jnp.dot(row_block, gate_weight, preferred_element_type=jnp.float32)
    up_part = jnp.dot(row_block, up_weight, preferred_element_type=jnp.float32)
    extra = adapt_in
    shares = lax.psum_scatter(
        (jnp.stack([gate_part, up_part], axis=1) + extra).astype(jnp.bfloat16),
        "tensor",
        scatter_dimension=0,
        tiled=True,
    ).astype(jnp.float32)
    hidden = (jax.nn.silu(shares[:, 0]) * shares[:, 1]).astype(jnp.bfloat16)
    hidden_all = lax.all_gather(hidden, "tensor", axis=0, tiled=True)
    projected_out = jnp.einsum(
        "tf,srf->tsr", hidden_all, adapter_proj_out, preferred_element_type=jnp.float32
    )
    rank_part_out = jnp.sum(
        projected_out * mask_store_tensor.astype(jnp.float32)[:, :, None], axis=1
    )
    rank_out = lax.psum(rank_part_out, ("dp", "tensor")).astype(jnp.bfloat16)
    spread_out = rank_out[:, None, :] * mask_store_dp[:, :, None]
    adapt_out = jnp.einsum(
        "tsr,srd->td", spread_out, adapter_lift_out, preferred_element_type=jnp.float32
    )
    row_block = hidden_all
    extra = adapt_out
    return lax.psum_scatter(
        (jnp.dot(row_block, down_weight, preferred_element_type=jnp.float32) + extra).astype(
            jnp.bfloat16
        ),
        "dp",
        scatter_dimension=0,
        tiled=True,
    )


OUTER = [(0, 1), (1, 0), (2, 3), (3, 2)]
MIDDLE = [(1, 2), (2, 1)]


def masked_project(block, rows, slot_row, first):
    slots, rank, depth = block.shape
    full = lax.dot_general(
        block.reshape(slots * rank, depth), rows, (((1,), (1,)), ((), ())), preferred_element_type=F32
    ).reshape(slots, rank, rows.shape[0])
    ids = first + lax.broadcasted_iota(jnp.int32, full.shape, 0)
    return jnp.sum(jnp.where(ids == slot_row[None], full, 0.0), axis=0)


def spread_rows(rank_t, slot_row, slots):
    rank, total = rank_t.shape
    width = slots * rank
    slot_col = jnp.broadcast_to(slot_row.astype(F32), (8, total)).T[:, :1].astype(jnp.int32)
    lane = lax.broadcasted_iota(jnp.int32, (rank, width), 1)
    row = lax.broadcasted_iota(jnp.int32, (rank, width), 0)
    copies = (lax.rem(lane, rank) == row).astype(F32).astype(BF16)
    tiled = lax.dot_general(
        rank_t.astype(F32).T.astype(BF16), copies, (((1,), (0,)), ((), ())), preferred_element_type=F32
    )
    owner = lax.div(lax.broadcasted_iota(jnp.int32, tiled.shape, 1), rank)
    return jnp.where(owner == slot_col, tiled, 0.0).astype(BF16)


IN_VMEM = pl.BlockSpec(memory_space=pltpu.VMEM)
IN_SMEM = pl.BlockSpec(memory_space=pltpu.SMEM)
ANYWHERE = pl.BlockSpec(memory_space=pl.ANY)
ROWS = 512
GROUP = 16


def call(kernel, name, in_specs, outs, scratch):
    return pl.pallas_call(
        kernel,
        in_specs=in_specs,
        out_specs=jax.tree.map(lambda _: IN_VMEM, outs),
        out_shape=outs,
        scratch_shapes=scratch,
        compiler_params=pltpu.CompilerParams(vmem_limit_bytes=VMEM_LIMIT),
        cost_estimate=LIGHT,
        name=name,
    )


def fetch(parts, sems):
    copies = [pltpu.make_async_copy(src, dst, sems.at[at]) for at, (src, dst) in enumerate(parts)]
    for copy in copies:
        copy.start()
    return copies


def rank_in_kernel(slot_ref, rows_ref, proj_ref, out_ref):
    step = pl.program_id(0)
    part = masked_project(proj_ref[...], rows_ref[...], slot_ref[...], step * proj_ref.shape[0])

    @pl.when(step == 0)
    def _():
        out_ref[...] = part

    @pl.when(step > 0)
    def _():
        out_ref[...] += part


def rank_in_call(slot_row, rows, proj):
    slots, rank, depth = proj.shape
    total = rows.shape[0]
    group = 8
    return pl.pallas_call(
        rank_in_kernel,
        grid=(slots // group,),
        in_specs=[
            pl.BlockSpec((1, total), lambda s: (0, 0)),
            pl.BlockSpec((total, depth), lambda s: (0, 0)),
            pl.BlockSpec((group, rank, depth), lambda s: (s, 0, 0)),
        ],
        out_specs=pl.BlockSpec((rank, total), lambda s: (0, 0)),
        out_shape=jax.ShapeDtypeStruct((rank, total), F32),
        compiler_params=pltpu.CompilerParams(vmem_limit_bytes=VMEM_LIMIT),
        cost_estimate=LIGHT,
        name="rank_in",
    )(slot_row, rows, proj)


def half_rows(side, which, half):
    start = side * half if which == 0 else (1 - side) * half
    return pl.ds(pl.multiple_of(start, 16), half)


def weight_parts(weight_ref, held_ref, first):
    blocks, rows, width = held_ref.shape
    return [
        (weight_ref.at[pl.ds(k * rows, rows), pl.ds(first * CELL, width)], held_ref.at[k]) for k in range(blocks)
    ]


def lift_parts(lift_ref, held_ref, first):
    groups, slots = held_ref.shape[:2]
    width = held_ref.shape[-1]
    return [
        (lift_ref.at[pl.ds(g * slots, slots), :, :, pl.ds(first * CELL, width)], held_ref.at[g])
        for g in range(groups)
    ]


def add_product(total_ref, fresh, left, right):
    product = jnp.dot(left, right, preferred_element_type=F32)
    total_ref[...] = product if fresh else total_ref[...] + product


def add_lift(total_ref, spread_ref, held_ref, g):
    _, slots, _, rank, width = held_ref.shape
    depth = slots * rank
    for c in range(2):
        left = spread_ref[c, :, g * depth:(g + 1) * depth]
        add_product(total_ref.at[c], False, left, held_ref[g, :, c].reshape(depth, width))


def halves_out(total_ref, side, near_ref, far_ref):
    half = near_ref.shape[1]
    for c in range(2):
        near_ref[c] = total_ref[c, half_rows(side, 0, half), :].astype(BF16)
        far_ref[c] = total_ref[c, half_rows(side, 1, half), :].astype(BF16)


def main_kernel(first, rows_ref, weight_ref, out_ref, held_ref, sems):
    copies = fetch(weight_parts(weight_ref, held_ref, first), sems)
    for k, copy in enumerate(copies):
        copy.wait()
        add_product(out_ref, k == 0, rows_ref[:, k * ROWS:(k + 1) * ROWS], held_ref[k])


def main_call(first, cells, rows, weight):
    total, depth = rows.shape
    blocks, width = depth // ROWS, cells * CELL
    return call(
        functools.partial(main_kernel, first),
        "main",
        [IN_VMEM, ANYWHERE],
        jax.ShapeDtypeStruct((total, width), F32),
        [pltpu.VMEM((blocks, ROWS, width), BF16), pltpu.SemaphoreType.DMA((blocks,))],
    )(rows, weight)


def first_kernel(side_ref, slot_ref, rank_ref, gate_ref, up_ref, lift_ref, near_ref, far_ref, spread_ref, total_ref, held_ref, sems):
    copies = fetch(lift_parts(lift_ref, held_ref, 0), sems)
    slots, _, rank, _ = lift_ref.shape
    for c, main_ref in ((0, gate_ref), (1, up_ref)):
        spread_ref[c] = spread_rows(rank_ref[c * rank:(c + 1) * rank, :], slot_ref[...], slots)
        total_ref[c] = main_ref[...]
    for g, copy in enumerate(copies):
        copy.wait()
        add_lift(total_ref, spread_ref, held_ref, g)
    halves_out(total_ref, side_ref[0], near_ref, far_ref)


def lift_held(lift, width):
    slots, two, rank, _ = lift.shape
    return pltpu.VMEM((slots // GROUP, GROUP, two, rank, width), BF16)


def first_call(side, slot_row, rank_t, gate, up, lift):
    slots, _, rank, _ = lift.shape
    total, width = gate.shape
    piece = jax.ShapeDtypeStruct((2, total // 2, width), BF16)
    return call(
        first_kernel,
        "first",
        [IN_SMEM] + [IN_VMEM] * 4 + [ANYWHERE],
        [piece, piece, jax.ShapeDtypeStruct((2, total, slots * rank), BF16)],
        [pltpu.VMEM((2, total, width), F32), lift_held(lift, width), pltpu.SemaphoreType.DMA((slots // GROUP,))],
    )(side, slot_row, rank_t, gate, up, lift)


def into_kernel(first, side_ref, rows_ref, spread_ref, gate_ref, up_ref, lift_ref, near_ref, far_ref, total_ref, gate_held, up_held, lift_buf, sems):
    blocks = gate_held.shape[0]
    parts = []
    for pair in zip(weight_parts(gate_ref, gate_held, first), weight_parts(up_ref, up_held, first)):
        parts += pair
    copies = fetch(parts + lift_parts(lift_ref, lift_buf, first), sems)
    for k in range(blocks):
        for c, held in ((0, gate_held), (1, up_held)):
            copies[2 * k + c].wait()
            add_product(total_ref.at[c], k == 0, rows_ref[:, k * ROWS:(k + 1) * ROWS], held[k])
    for g, copy in enumerate(copies[2 * blocks:]):
        copy.wait()
        add_lift(total_ref, spread_ref, lift_buf, g)
    halves_out(total_ref, side_ref[0], near_ref, far_ref)


def into_call(first, cells, side, spread, rows, gate_weight, up_weight, lift):
    total, depth = rows.shape
    blocks, width = depth // ROWS, cells * CELL
    held = pltpu.VMEM((blocks, ROWS, width), BF16)
    return call(
        functools.partial(into_kernel, first),
        "into",
        [IN_SMEM, IN_VMEM, IN_VMEM] + [ANYWHERE] * 3,
        [jax.ShapeDtypeStruct((2, total // 2, width), BF16)] * 2,
        [
            pltpu.VMEM((2, total, width), F32),
            held,
            held,
            lift_held(lift, width),
            pltpu.SemaphoreType.DMA((2 * blocks + lift.shape[0] // GROUP,)),
        ],
    )(side, rows, spread, gate_weight, up_weight, lift)


def whole_hidden(side, near_ref, far_ref, hidden_ref):
    half = near_ref.shape[0]
    hidden_ref[half_rows(side, 0, half), :] = near_ref[...]
    hidden_ref[half_rows(side, 1, half), :] = far_ref[...]


def project_parts(proj_ref, held_ref, first):
    groups, slots = held_ref.shape[:2]
    columns = pl.ds(first * CELL, held_ref.shape[-1])
    return [(proj_ref.at[pl.ds(g * slots, slots), :, columns], held_ref.at[g]) for g in range(groups)]


def project_kernel(first, later, side_ref, slot_ref, near_ref, far_ref, proj_ref, before_ref, out_ref, brought_ref, hidden_ref, held_ref, sems):
    parts = project_parts(proj_ref, held_ref, first)
    copies = fetch(parts + project_parts(proj_ref, brought_ref, later) * (later > 0), sems)
    whole_hidden(side_ref[0], near_ref, far_ref, hidden_ref)
    total = before_ref[...]
    slots = held_ref.shape[1]
    for g in range(len(parts)):
        copies[g].wait()
        total += masked_project(held_ref[g], hidden_ref[...], slot_ref[...], g * slots)
    out_ref[...] = total
    for copy in copies[len(parts):]:
        copy.wait()


def project_call(first, later, later_cells, side, slot_row, parts, proj, carried):
    slots, rank, _ = proj.shape
    half, width = parts[0].shape
    groups = slots // GROUP
    held = (groups, GROUP, rank)
    return call(
        functools.partial(project_kernel, first, later),
        "project",
        [IN_SMEM] + [IN_VMEM] * 3 + [ANYWHERE, IN_VMEM],
        [
            jax.ShapeDtypeStruct((rank, 2 * half), F32),
            jax.ShapeDtypeStruct((*held, later_cells * CELL), BF16),
        ],
        [
            pltpu.VMEM((2 * half, width), BF16),
            pltpu.VMEM((*held, width), BF16),
            pltpu.SemaphoreType.DMA((2 * groups,)),
        ],
    )(side, slot_row, *parts, proj, carried)


def project_last_kernel(side_ref, slot_ref, near_ref, far_ref, held_ref, before_ref, out_ref, hidden_ref):
    whole_hidden(side_ref[0], near_ref, far_ref, hidden_ref)
    total = before_ref[...]
    slots = held_ref.shape[1]
    for g in range(held_ref.shape[0]):
        total += masked_project(held_ref[g], hidden_ref[...], slot_ref[...], g * slots)
    out_ref[...] = total


def project_last_call(side, slot_row, parts, held, carried):
    half, width = parts[0].shape
    return call(
        project_last_kernel,
        "project",
        [IN_SMEM] + [IN_VMEM] * 5,
        jax.ShapeDtypeStruct(carried.shape, F32),
        [pltpu.VMEM((2 * half, width), BF16)],
    )(side, slot_row, *parts, held, carried)


def down_kernel(first, bring, side_ref, near_ref, far_ref, down_ref, *rest):
    rest, (hidden_ref, held_ref, sems) = rest[:-3], rest[-3:]
    if bring:
        rest, (later_ref, out_ref, brought_ref) = rest[:-3], rest[-3:]
    else:
        rest, out_ref = rest[:-1], rest[-1]
    cells = held_ref.shape[0]
    parts = [(down_ref.at[pl.ds((first + k) * CELL, CELL), :], held_ref.at[k]) for k in range(cells)]
    if bring:
        parts.append((later_ref, brought_ref))
    copies = fetch(parts, sems)
    whole_hidden(side_ref[0], near_ref, far_ref, hidden_ref)
    for k in range(cells):
        copies[k].wait()
        product = jnp.dot(hidden_ref[:, k * CELL:(k + 1) * CELL], held_ref[k], preferred_element_type=F32)
        if k > 0:
            product += out_ref[...]
        elif rest:
            product += rest[0][...]
        out_ref[...] = product
    if bring:
        copies[cells].wait()


def down_call(first, side, parts, down, carried, later=None):
    half, width = parts[0].shape
    out = down.shape[1]
    cells = width // CELL
    extra = () if carried is None else (carried,)
    bring = () if later is None else (later,)
    sums = jax.ShapeDtypeStruct((2 * half, out), F32)
    return call(
        functools.partial(down_kernel, first, len(bring)),
        "down",
        [IN_SMEM, IN_VMEM, IN_VMEM, ANYWHERE] + [IN_VMEM for _ in extra] + [ANYWHERE for _ in bring],
        [sums, jax.ShapeDtypeStruct(later.shape, later.dtype)] if bring else sums,
        [
            pltpu.VMEM((2 * half, width), BF16),
            pltpu.VMEM((cells, CELL, out), BF16),
            pltpu.SemaphoreType.DMA((cells + len(bring),)),
        ],
    )(side, *parts, down, *extra, *bring)


def last_kernel(slot_ref, rank_ref, sum_ref, lift_ref, out_ref):
    slots, rank, width = lift_ref.shape
    spread = spread_rows(rank_ref[...], slot_ref[...], slots)
    extra = jnp.dot(spread, lift_ref[...].reshape(slots * rank, width), preferred_element_type=F32)
    out_ref[...] = (sum_ref[...] + extra).astype(BF16)


def last_call(slot_row, rank_t, sums, lift):
    return call(
        last_kernel, "last", [IN_VMEM] * 4, jax.ShapeDtypeStruct(sums.shape, BF16), []
    )(slot_row, rank_t, sums, lift)


def after(value, *behind):
    return lax.optimization_barrier((value, *behind))[0]


def swap(value, axis, size, mask):
    return lax.ppermute(value, axis, [(i, i ^ mask) for i in range(size)])


def gather_dp(block, beside):
    me = lax.axis_index("dp")
    chip = me >> 1
    near = jnp.stack([block] + [swap(block, "dp", 8, 2 * mask) for mask in (1, 2, 3)])
    near, beside = lax.optimization_barrier((near, beside))
    other = swap(near, "dp", 8, 1)
    both = jnp.where((me & 1) == 0, jnp.stack([near, other], 1), jnp.stack([other, near], 1))
    both = jnp.where((chip & 1) == 0, both, jnp.stack([both[1], both[0], both[3], both[2]]))
    both = jnp.where((chip & 2) == 0, both, jnp.stack([both[2], both[3], both[0], both[1]]))
    return both.reshape(8 * block.shape[0], block.shape[1]), beside


def sum_everywhere(value, beside=()):
    made = []
    for stage, (axis, size, masks) in enumerate(
        (("dp", 8, (1,)), ("dp", 8, (6, 2, 4)), ("tensor", 4, (1,)), ("tensor", 4, (2,)))
    ):
        others = [swap(value, axis, size, mask) for mask in masks]
        for when, work in beside:
            if when == stage:
                made.append(work(value, *made[-1:]))
                others, made[-1] = lax.optimization_barrier((others, made[-1]))
        value = sum(others, value)
    return value, made


def scatter_dp(rows):
    total, width = rows.shape
    me = lax.axis_index("dp")
    core = me & 1
    blocks = rows.reshape(4, 2, total // 8, width)
    mine = lax.dynamic_index_in_dim(blocks, core, 1, keepdims=False)
    other = lax.dynamic_index_in_dim(blocks, 1 - core, 1, keepdims=False)
    both = (mine.astype(F32) + swap(other, "dp", 8, 1).astype(F32)).astype(BF16)
    chip = me >> 1
    kept = lax.dynamic_index_in_dim(both, chip, 0, keepdims=False).astype(F32)
    for mask in (3, 1, 2):
        sent = lax.dynamic_index_in_dim(both, chip ^ mask, 0, keepdims=False)
        kept = kept + swap(sent, "dp", 8, 2 * mask).astype(F32)
    return kept.astype(BF16)


def line_device(
    tokens,
    gate_weight,
    up_weight,
    down_weight,
    adapter_proj_in,
    adapter_lift_in,
    adapter_proj_out,
    adapter_lift_out,
    token_request,
    request_adapter,
    adapter_slot,
):
    slot_of = lookup(lookup(token_request, request_adapter), adapter_slot)
    gathered, slot_of = gather_dp(tokens, slot_of)
    dp_index = lax.axis_index("dp")
    tensor_index = lax.axis_index("tensor")
    side = (tensor_index >> 1).astype(jnp.int32).reshape(1)
    is_end = (tensor_index == 0) | (tensor_index == 3)
    slot_dp = slot_of - dp_index * adapter_proj_in.shape[0]
    slot_tensor = slot_of - tensor_index * adapter_lift_in.shape[0]
    rank_part = rank_in_call(slot_dp[None, :], gathered, adapter_proj_in)
    rank_in, mains = sum_everywhere(
        rank_part,
        [
            (1, lambda tie: main_call(0, CHUNKS[0], after(gathered, tie), gate_weight)),
            (2, lambda tie, before: main_call(0, CHUNKS[0], after(gathered, tie, before), up_weight)),
        ],
    )
    rank_in = rank_in.astype(BF16)
    slot_row = slot_tensor[None, :]
    chunks = len(CHUNKS)
    starts = [sum(CHUNKS[:c]) for c in range(chunks)]
    near, far, hop, hidden_near, hidden_far = ({} for _ in range(5))

    def operand(c, stage):
        if stage == 0:
            return far[c]
        if stage == 1:
            return (far[c].astype(F32) + hop[c].astype(F32)).astype(BF16)
        if stage == 2:
            return (near[c].astype(F32) + hop[c].astype(F32)).astype(BF16)
        if stage == 3:
            both = near[c].astype(F32) + hop[c].astype(F32)
            hidden_near[c] = (jax.nn.silu(both[0]) * both[1]).astype(BF16)[None]
            return hidden_near[c]
        if stage == 4:
            hidden_near[c] = jnp.where(is_end, hidden_near[c], hop[c])
            return hop[c]
        hidden_far[c] = hop[c]
        return hop[c]

    def pair(c):
        return [hidden_near[c][0], jnp.where(is_end, hop[c], hidden_far[c])[0]]

    def padded(value, shape):
        return jnp.pad(value, [(0, b - a) for a, b in zip(value.shape, shape)])

    near[0], far[0], spread = first_call(side, slot_row, rank_in, *mains, adapter_lift_in)
    sums, ranks = None, None
    for slot in range(chunks + 5):
        live = [(slot - stage, stage) for stage in range(6) if 0 <= slot - stage < chunks]
        values = {stage % 3: operand(c, stage) for c, stage in live}
        if 0 in values and 2 in values:
            shape = tuple(max(a, b) for a, b in zip(values[0].shape, values[2].shape))
            outer = jnp.where(is_end, padded(values[0], shape), padded(values[2], shape))
        else:
            outer = values.get(0, values.get(2))
        sent = [value for value in (outer, values.get(1)) if value is not None]
        sent = list(lax.optimization_barrier(tuple(sent)))
        arrived = {}
        if outer is not None:
            arrived[0] = lax.ppermute(sent[0], "tensor", OUTER)
        if 1 in values:
            arrived[1] = lax.ppermute(sent[-1], "tensor", MIDDLE)
        made = ()
        if slot + 1 < chunks:
            made = into_call(
                starts[slot + 1], CHUNKS[slot + 1], after(side, *sent), spread, gathered, gate_weight, up_weight, adapter_lift_in
            )
        done = slot - 6
        if done == 0:
            early = pair(0)
            zero = jnp.zeros((adapter_proj_out.shape[1], gathered.shape[0]), F32)
            ranks, _ = project_call(starts[0], 0, 1, after(side, *sent), slot_row, early, adapter_proj_out, zero)
            sums = down_call(starts[0], after(side, ranks), early, down_weight, None)
            made = (ranks, sums)
        elif done > 0:
            ranks, ahead = project_call(
                starts[1], starts[2], CHUNKS[2], after(side, *sent), slot_row, pair(1), adapter_proj_out, ranks
            )
            made = (ranks, ahead)
        *came, = lax.optimization_barrier((*arrived.values(), *made))
        arrived = dict(zip(arrived, came))
        made = came[len(arrived):]
        if slot + 1 < chunks:
            near[slot + 1], far[slot + 1] = made
        elif done == 0:
            ranks, sums = made
        elif done > 0:
            ranks, ahead = made
        for c, stage in live:
            value = arrived[stage % 3 % 2]
            units, width = (2, 1)[stage // 3], CHUNKS[c] * CELL
            hop[c] = value[:units, :, :width]
    ranks = project_last_call(side, slot_row, pair(2), ahead, ranks)
    rank_out, made = sum_everywhere(
        ranks,
        [
            (1, lambda tie: down_call(starts[1], after(side, tie), pair(1), down_weight, sums, adapter_lift_out)),
            (2, lambda tie, before: (down_call(starts[2], after(side, tie), pair(2), down_weight, before[0]), before[1])),
        ],
    )
    return scatter_dp(last_call(slot_dp[None, :], rank_out.astype(BF16), *made[-1]))


def solution(mesh):
    on_line = mesh.shape["tensor"] == 4 and mesh.shape["dp"] == 8
    placed = (
        P("dp", "tensor"),
        P("tensor", "dp"),
        P("tensor", "dp"),
        P("dp", "tensor"),
        P("dp", None, "tensor"),
        P("tensor", None, None, "dp"),
        P("tensor", None, "dp"),
        P("dp", None, "tensor"),
        P(),
        P(),
        P(),
    )
    return jax.shard_map(
        line_device if on_line else general_device, mesh=mesh, in_specs=placed, out_specs=P("dp", "tensor"), check_vma=False
    )
```

```python
import functools

import jax
import jax.numpy as jnp
from jax import lax
from jax.experimental import pallas as pl
from jax.experimental.pallas import tpu as pltpu
from jax.sharding import PartitionSpec as P

CELL = 256
CHUNKS = (4, 5, 5)
VMEM_LIMIT = 40 << 20
LIGHT = pl.CostEstimate(flops=1024, bytes_accessed=1024, transcendentals=0)
F32 = jnp.float32
BF16 = jnp.bfloat16


def lookup(keys, table):
    hits = keys[:, None] == jnp.arange(table.shape[0], dtype=jnp.int32)[None, :]
    return jnp.sum(jnp.where(hits, table[None, :], 0), axis=1)


def owned(slot_of, first_slot, amount):
    places = first_slot + jnp.arange(amount, dtype=jnp.int32)
    return (slot_of[:, None] == places[None, :]).astype(jnp.bfloat16)


def general_device(
    tokens,
    gate_weight,
    up_weight,
    down_weight,
    adapter_proj_in,
    adapter_lift_in,
    adapter_proj_out,
    adapter_lift_out,
    token_request,
    request_adapter,
    adapter_slot,
):
    slot_of = lookup(lookup(token_request, request_adapter), adapter_slot)
    dp_index = lax.axis_index("dp")
    tensor_index = lax.axis_index("tensor")
    per_dp = adapter_proj_in.shape[0]
    per_tensor = adapter_lift_in.shape[0]
    rank = adapter_lift_out.shape[1]
    gathered = lax.all_gather(tokens, "dp", axis=0, tiled=True)
    total_rows = gathered.shape[0]
    mask_store_dp = owned(slot_of, dp_index * per_dp, per_dp)
    mask_store_tensor = owned(slot_of, tensor_index * per_tensor, per_tensor)
    projected = jnp.einsum(
        "td,srd->tsr", gathered, adapter_proj_in, preferred_element_type=jnp.float32
    )
    rank_part = jnp.sum(projected * mask_store_dp.astype(jnp.float32)[:, :, None], axis=1)
    rank_in = lax.psum(rank_part, ("dp", "tensor")).astype(jnp.bfloat16)
    rank_in = rank_in.reshape(total_rows, 2, rank)
    spread = rank_in[:, None, :, :] * mask_store_tensor[:, :, None, None]
    adapt_in = jnp.einsum(
        "tscr,scrf->tcf", spread, adapter_lift_in, preferred_element_type=jnp.float32
    )
    row_block = gathered
    gate_part = jnp.dot(row_block, gate_weight, preferred_element_type=jnp.float32)
    up_part = jnp.dot(row_block, up_weight, preferred_element_type=jnp.float32)
    extra = adapt_in
    shares = lax.psum_scatter(
        (jnp.stack([gate_part, up_part], axis=1) + extra).astype(jnp.bfloat16),
        "tensor",
        scatter_dimension=0,
        tiled=True,
    ).astype(jnp.float32)
    hidden = (jax.nn.silu(shares[:, 0]) * shares[:, 1]).astype(jnp.bfloat16)
    hidden_all = lax.all_gather(hidden, "tensor", axis=0, tiled=True)
    projected_out = jnp.einsum(
        "tf,srf->tsr", hidden_all, adapter_proj_out, preferred_element_type=jnp.float32
    )
    rank_part_out = jnp.sum(
        projected_out * mask_store_tensor.astype(jnp.float32)[:, :, None], axis=1
    )
    rank_out = lax.psum(rank_part_out, ("dp", "tensor")).astype(jnp.bfloat16)
    spread_out = rank_out[:, None, :] * mask_store_dp[:, :, None]
    adapt_out = jnp.einsum(
        "tsr,srd->td", spread_out, adapter_lift_out, preferred_element_type=jnp.float32
    )
    row_block = hidden_all
    extra = adapt_out
    return lax.psum_scatter(
        (jnp.dot(row_block, down_weight, preferred_element_type=jnp.float32) + extra).astype(
            jnp.bfloat16
        ),
        "dp",
        scatter_dimension=0,
        tiled=True,
    )


OUTER = [(0, 1), (1, 0), (2, 3), (3, 2)]
MIDDLE = [(1, 2), (2, 1)]


def masked_project(block, rows, slot_row, first):
    slots, rank, depth = block.shape
    full = lax.dot_general(
        block.reshape(slots * rank, depth), rows, (((1,), (1,)), ((), ())), preferred_element_type=F32
    ).reshape(slots, rank, rows.shape[0])
    ids = first + lax.broadcasted_iota(jnp.int32, full.shape, 0)
    return jnp.sum(jnp.where(ids == slot_row[None], full, 0.0), axis=0)


def spread_rows(rank_t, slot_row, slots):
    rank, total = rank_t.shape
    width = slots * rank
    slot_col = jnp.broadcast_to(slot_row.astype(F32), (8, total)).T[:, :1].astype(jnp.int32)
    lane = lax.broadcasted_iota(jnp.int32, (rank, width), 1)
    row = lax.broadcasted_iota(jnp.int32, (rank, width), 0)
    copies = (lax.rem(lane, rank) == row).astype(F32).astype(BF16)
    tiled = lax.dot_general(
        rank_t.astype(F32).T.astype(BF16), copies, (((1,), (0,)), ((), ())), preferred_element_type=F32
    )
    owner = lax.div(lax.broadcasted_iota(jnp.int32, tiled.shape, 1), rank)
    return jnp.where(owner == slot_col, tiled, 0.0).astype(BF16)


IN_VMEM = pl.BlockSpec(memory_space=pltpu.VMEM)
IN_SMEM = pl.BlockSpec(memory_space=pltpu.SMEM)
ANYWHERE = pl.BlockSpec(memory_space=pl.ANY)
ROWS = 512
GROUP = 16


def call(kernel, name, in_specs, outs, scratch):
    return pl.pallas_call(
        kernel,
        in_specs=in_specs,
        out_specs=jax.tree.map(lambda _: IN_VMEM, outs),
        out_shape=outs,
        scratch_shapes=scratch,
        compiler_params=pltpu.CompilerParams(vmem_limit_bytes=VMEM_LIMIT),
        cost_estimate=LIGHT,
        name=name,
    )


def fetch(parts, sems):
    copies = [pltpu.make_async_copy(src, dst, sems.at[at]) for at, (src, dst) in enumerate(parts)]
    for copy in copies:
        copy.start()
    return copies


def rank_in_kernel(slot_ref, rows_ref, proj_ref, out_ref):
    out_ref[...] = masked_project(proj_ref[...], rows_ref[...], slot_ref[...], 0)


def rank_in_call(slot_row, rows, proj):
    outs = jax.ShapeDtypeStruct((proj.shape[1], rows.shape[0]), F32)
    return call(rank_in_kernel, "rank_in", [IN_VMEM] * 3, outs, [])(slot_row, rows, proj)


def half_rows(side, which, half):
    start = side * half if which == 0 else (1 - side) * half
    return pl.ds(pl.multiple_of(start, 16), half)


def weight_parts(weight_ref, held_ref, first):
    blocks, rows, width = held_ref.shape
    return [
        (weight_ref.at[pl.ds(k * rows, rows), pl.ds(first * CELL, width)], held_ref.at[k]) for k in range(blocks)
    ]


def lift_parts(lift_ref, held_ref, first):
    groups, slots = held_ref.shape[:2]
    width = held_ref.shape[-1]
    return [
        (lift_ref.at[pl.ds(g * slots, slots), :, :, pl.ds(first * CELL, width)], held_ref.at[g])
        for g in range(groups)
    ]


def add_product(total_ref, fresh, left, right):
    product = jnp.dot(left, right, preferred_element_type=F32)
    total_ref[...] = product if fresh else total_ref[...] + product


def add_lift(total_ref, spread_ref, held_ref, g):
    _, slots, _, rank, width = held_ref.shape
    depth = slots * rank
    for c in range(2):
        left = spread_ref[c, :, g * depth:(g + 1) * depth]
        add_product(total_ref.at[c], False, left, held_ref[g, :, c].reshape(depth, width))


def halves_out(total_ref, side, near_ref, far_ref):
    half = near_ref.shape[1]
    for c in range(2):
        near_ref[c] = total_ref[c, half_rows(side, 0, half), :].astype(BF16)
        far_ref[c] = total_ref[c, half_rows(side, 1, half), :].astype(BF16)


def main_kernel(first, rows_ref, weight_ref, out_ref, held_ref, sems):
    copies = fetch(weight_parts(weight_ref, held_ref, first), sems)
    for k, copy in enumerate(copies):
        copy.wait()
        add_product(out_ref, k == 0, rows_ref[:, k * ROWS:(k + 1) * ROWS], held_ref[k])


def main_call(first, cells, rows, weight):
    total, depth = rows.shape
    blocks, width = depth // ROWS, cells * CELL
    return call(
        functools.partial(main_kernel, first),
        "main",
        [IN_VMEM, ANYWHERE],
        jax.ShapeDtypeStruct((total, width), F32),
        [pltpu.VMEM((blocks, ROWS, width), BF16), pltpu.SemaphoreType.DMA((blocks,))],
    )(rows, weight)


def first_kernel(side_ref, slot_ref, rank_ref, gate_ref, up_ref, lift_ref, near_ref, far_ref, spread_ref, total_ref, held_ref, sems):
    copies = fetch(lift_parts(lift_ref, held_ref, 0), sems)
    slots, _, rank, _ = lift_ref.shape
    for c, main_ref in ((0, gate_ref), (1, up_ref)):
        spread_ref[c] = spread_rows(rank_ref[c * rank:(c + 1) * rank, :], slot_ref[...], slots)
        total_ref[c] = main_ref[...]
    for g, copy in enumerate(copies):
        copy.wait()
        add_lift(total_ref, spread_ref, held_ref, g)
    halves_out(total_ref, side_ref[0], near_ref, far_ref)


def lift_held(lift, width):
    slots, two, rank, _ = lift.shape
    return pltpu.VMEM((slots // GROUP, GROUP, two, rank, width), BF16)


def first_call(side, slot_row, rank_t, gate, up, lift):
    slots, _, rank, _ = lift.shape
    total, width = gate.shape
    piece = jax.ShapeDtypeStruct((2, total // 2, width), BF16)
    return call(
        first_kernel,
        "first",
        [IN_SMEM] + [IN_VMEM] * 4 + [ANYWHERE],
        [piece, piece, jax.ShapeDtypeStruct((2, total, slots * rank), BF16)],
        [pltpu.VMEM((2, total, width), F32), lift_held(lift, width), pltpu.SemaphoreType.DMA((slots // GROUP,))],
    )(side, slot_row, rank_t, gate, up, lift)


def into_kernel(first, ready, side_ref, rows_ref, spread_ref, gate_ref, up_ref, lift_ref, near_ref, far_ref, total_ref, held_ref, lift_buf, sems):
    gates = [(gate_ref, total_ref.at[0])] if ready else weight_parts(gate_ref, held_ref.at[1], first)
    ups = weight_parts(up_ref, held_ref.at[0], first)
    lifts = lift_parts(lift_ref, lift_buf, first)
    copies = fetch(gates + ups + lifts, sems)
    at = 0
    for c, count in ((0, len(gates)), (1, len(ups))):
        for k in range(count):
            copies[at].wait()
            at += 1
            if c == 1 or not ready:
                add_product(total_ref.at[c], k == 0, rows_ref[:, k * ROWS:(k + 1) * ROWS], held_ref[1 - c, k])
    for g, copy in enumerate(copies[at:]):
        copy.wait()
        add_lift(total_ref, spread_ref, lift_buf, g)
    halves_out(total_ref, side_ref[0], near_ref, far_ref)


def into_call(first, cells, side, spread, rows, gate, up_weight, lift, ready):
    total, depth = rows.shape
    blocks, width = depth // ROWS, cells * CELL
    copies = (1 if ready else blocks) + blocks + lift.shape[0] // GROUP
    return call(
        functools.partial(into_kernel, first, ready),
        "into",
        [IN_SMEM, IN_VMEM, IN_VMEM] + [ANYWHERE] * 3,
        [jax.ShapeDtypeStruct((2, total // 2, width), BF16)] * 2,
        [
            pltpu.VMEM((2, total, width), F32),
            pltpu.VMEM((1 if ready else 2, blocks, ROWS, width), BF16),
            lift_held(lift, width),
            pltpu.SemaphoreType.DMA((copies,)),
        ],
    )(side, rows, spread, gate, up_weight, lift)


def whole_hidden(side, near_ref, far_ref, hidden_ref):
    half = near_ref.shape[0]
    hidden_ref[half_rows(side, 0, half), :] = near_ref[...]
    hidden_ref[half_rows(side, 1, half), :] = far_ref[...]


def project_parts(proj_ref, held_ref, first):
    groups, slots = held_ref.shape[:2]
    columns = pl.ds(first * CELL, held_ref.shape[-1])
    return [(proj_ref.at[pl.ds(g * slots, slots), :, columns], held_ref.at[g]) for g in range(groups)]


def project_kernel(first, later, side_ref, slot_ref, near_ref, far_ref, proj_ref, before_ref, out_ref, brought_ref, hidden_ref, held_ref, sems):
    parts = project_parts(proj_ref, held_ref, first)
    copies = fetch(parts + project_parts(proj_ref, brought_ref, later) * (later > 0), sems)
    whole_hidden(side_ref[0], near_ref, far_ref, hidden_ref)
    total = before_ref[...]
    slots = held_ref.shape[1]
    for g in range(len(parts)):
        copies[g].wait()
        total += masked_project(held_ref[g], hidden_ref[...], slot_ref[...], g * slots)
    out_ref[...] = total
    for copy in copies[len(parts):]:
        copy.wait()


def project_call(first, later, later_cells, side, slot_row, parts, proj, carried):
    slots, rank, _ = proj.shape
    half, width = parts[0].shape
    groups = slots // GROUP
    held = (groups, GROUP, rank)
    return call(
        functools.partial(project_kernel, first, later),
        "project",
        [IN_SMEM] + [IN_VMEM] * 3 + [ANYWHERE, IN_VMEM],
        [
            jax.ShapeDtypeStruct((rank, 2 * half), F32),
            jax.ShapeDtypeStruct((*held, later_cells * CELL), BF16),
        ],
        [
            pltpu.VMEM((2 * half, width), BF16),
            pltpu.VMEM((*held, width), BF16),
            pltpu.SemaphoreType.DMA((2 * groups,)),
        ],
    )(side, slot_row, *parts, proj, carried)


def project_last_kernel(side_ref, slot_ref, near_ref, far_ref, held_ref, before_ref, out_ref, hidden_ref):
    whole_hidden(side_ref[0], near_ref, far_ref, hidden_ref)
    total = before_ref[...]
    slots = held_ref.shape[1]
    for g in range(held_ref.shape[0]):
        total += masked_project(held_ref[g], hidden_ref[...], slot_ref[...], g * slots)
    out_ref[...] = total


def project_last_call(side, slot_row, parts, held, carried):
    half, width = parts[0].shape
    return call(
        project_last_kernel,
        "project",
        [IN_SMEM] + [IN_VMEM] * 5,
        jax.ShapeDtypeStruct(carried.shape, F32),
        [pltpu.VMEM((2 * half, width), BF16)],
    )(side, slot_row, *parts, held, carried)


def down_kernel(first, bring, side_ref, near_ref, far_ref, down_ref, *rest):
    rest, (hidden_ref, held_ref, sems) = rest[:-3], rest[-3:]
    if bring:
        rest, (later_ref, out_ref, brought_ref) = rest[:-3], rest[-3:]
    else:
        rest, out_ref = rest[:-1], rest[-1]
    cells = held_ref.shape[0]
    parts = [(down_ref.at[pl.ds((first + k) * CELL, CELL), :], held_ref.at[k]) for k in range(cells)]
    if bring:
        parts.append((later_ref, brought_ref))
    copies = fetch(parts, sems)
    whole_hidden(side_ref[0], near_ref, far_ref, hidden_ref)
    for k in range(cells):
        copies[k].wait()
        product = jnp.dot(hidden_ref[:, k * CELL:(k + 1) * CELL], held_ref[k], preferred_element_type=F32)
        if k > 0:
            product += out_ref[...]
        elif rest:
            product += rest[0][...]
        out_ref[...] = product
    if bring:
        copies[cells].wait()


def down_call(first, side, parts, down, carried, later=None):
    half, width = parts[0].shape
    out = down.shape[1]
    cells = width // CELL
    extra = () if carried is None else (carried,)
    bring = () if later is None else (later,)
    sums = jax.ShapeDtypeStruct((2 * half, out), F32)
    return call(
        functools.partial(down_kernel, first, len(bring)),
        "down",
        [IN_SMEM, IN_VMEM, IN_VMEM, ANYWHERE] + [IN_VMEM for _ in extra] + [ANYWHERE for _ in bring],
        [sums, jax.ShapeDtypeStruct(later.shape, later.dtype)] if bring else sums,
        [
            pltpu.VMEM((2 * half, width), BF16),
            pltpu.VMEM((cells, CELL, out), BF16),
            pltpu.SemaphoreType.DMA((cells + len(bring),)),
        ],
    )(side, *parts, down, *extra, *bring)


def last_kernel(slot_ref, rank_ref, sum_ref, lift_ref, out_ref):
    slots, rank, width = lift_ref.shape
    spread = spread_rows(rank_ref[...], slot_ref[...], slots)
    extra = jnp.dot(spread, lift_ref[...].reshape(slots * rank, width), preferred_element_type=F32)
    out_ref[...] = (sum_ref[...] + extra).astype(BF16)


def last_call(slot_row, rank_t, sums, lift):
    return call(
        last_kernel, "last", [IN_VMEM] * 4, jax.ShapeDtypeStruct(sums.shape, BF16), []
    )(slot_row, rank_t, sums, lift)


def after(value, *behind):
    return lax.optimization_barrier((value, *behind))[0]


def swap(value, axis, size, mask):
    return lax.ppermute(value, axis, [(i, i ^ mask) for i in range(size)])


def gather_dp(block, beside):
    me = lax.axis_index("dp")
    chip = me >> 1
    near = jnp.stack([block] + [swap(block, "dp", 8, 2 * mask) for mask in (1, 2, 3)])
    near, beside = lax.optimization_barrier((near, beside))
    other = swap(near, "dp", 8, 1)
    both = jnp.where((me & 1) == 0, jnp.stack([near, other], 1), jnp.stack([other, near], 1))
    both = jnp.where((chip & 1) == 0, both, jnp.stack([both[1], both[0], both[3], both[2]]))
    both = jnp.where((chip & 2) == 0, both, jnp.stack([both[2], both[3], both[0], both[1]]))
    return both.reshape(8 * block.shape[0], block.shape[1]), beside


def sum_everywhere(value, beside=()):
    made = []
    for stage, (axis, size, masks) in enumerate(
        (("dp", 8, (1,)), ("dp", 8, (6, 2, 4)), ("tensor", 4, (1,)), ("tensor", 4, (2,)))
    ):
        others = [swap(value, axis, size, mask) for mask in masks]
        for when, work in beside:
            if when == stage:
                made.append(work(value, *made[-1:]))
                others, made[-1] = lax.optimization_barrier((others, made[-1]))
        value = sum(others, value)
    return value, made


def scatter_dp(rows):
    total, width = rows.shape
    me = lax.axis_index("dp")
    core = me & 1
    blocks = rows.reshape(4, 2, total // 8, width)
    mine = lax.dynamic_index_in_dim(blocks, core, 1, keepdims=False)
    other = lax.dynamic_index_in_dim(blocks, 1 - core, 1, keepdims=False)
    both = (mine.astype(F32) + swap(other, "dp", 8, 1).astype(F32)).astype(BF16)
    chip = me >> 1
    kept = lax.dynamic_index_in_dim(both, chip, 0, keepdims=False).astype(F32)
    for mask in (3, 1, 2):
        sent = lax.dynamic_index_in_dim(both, chip ^ mask, 0, keepdims=False)
        kept = kept + swap(sent, "dp", 8, 2 * mask).astype(F32)
    return kept.astype(BF16)


def line_device(
    tokens,
    gate_weight,
    up_weight,
    down_weight,
    adapter_proj_in,
    adapter_lift_in,
    adapter_proj_out,
    adapter_lift_out,
    token_request,
    request_adapter,
    adapter_slot,
):
    slot_of = lookup(lookup(token_request, request_adapter), adapter_slot)
    gathered, slot_of = gather_dp(tokens, slot_of)
    dp_index = lax.axis_index("dp")
    tensor_index = lax.axis_index("tensor")
    side = (tensor_index >> 1).astype(jnp.int32).reshape(1)
    is_end = (tensor_index == 0) | (tensor_index == 3)
    slot_dp = slot_of - dp_index * adapter_proj_in.shape[0]
    slot_tensor = slot_of - tensor_index * adapter_lift_in.shape[0]
    rank_part = rank_in_call(slot_dp[None, :], gathered, adapter_proj_in)
    rank_in, mains = sum_everywhere(
        rank_part,
        [
            (1, lambda tie: main_call(0, CHUNKS[0], after(gathered, tie), gate_weight)),
            (2, lambda tie, before: main_call(0, CHUNKS[0], after(gathered, tie, before), up_weight)),
        ],
    )
    rank_in = rank_in.astype(BF16)
    slot_row = slot_tensor[None, :]
    chunks = len(CHUNKS)
    starts = [sum(CHUNKS[:c]) for c in range(chunks)]
    near, far, hop, hidden_near, hidden_far = ({} for _ in range(5))

    def operand(c, stage):
        if stage == 0:
            return far[c]
        if stage == 1:
            return (far[c].astype(F32) + hop[c].astype(F32)).astype(BF16)
        if stage == 2:
            return (near[c].astype(F32) + hop[c].astype(F32)).astype(BF16)
        if stage == 3:
            both = near[c].astype(F32) + hop[c].astype(F32)
            hidden_near[c] = (jax.nn.silu(both[0]) * both[1]).astype(BF16)[None]
            return hidden_near[c]
        if stage == 4:
            hidden_near[c] = jnp.where(is_end, hidden_near[c], hop[c])
            return hop[c]
        hidden_far[c] = hop[c]
        return hop[c]

    def pair(c):
        return [hidden_near[c][0], jnp.where(is_end, hop[c], hidden_far[c])[0]]

    def padded(value, shape):
        return jnp.pad(value, [(0, b - a) for a, b in zip(value.shape, shape)])

    near[0], far[0], spread = first_call(side, slot_row, rank_in, *mains[:2], adapter_lift_in)
    sums, ranks = None, None
    for slot in range(chunks + 5):
        live = [(slot - stage, stage) for stage in range(6) if 0 <= slot - stage < chunks]
        values = {stage % 3: operand(c, stage) for c, stage in live}
        if 0 in values and 2 in values:
            shape = tuple(max(a, b) for a, b in zip(values[0].shape, values[2].shape))
            outer = jnp.where(is_end, padded(values[0], shape), padded(values[2], shape))
        else:
            outer = values.get(0, values.get(2))
        sent = [value for value in (outer, values.get(1)) if value is not None]
        sent = list(lax.optimization_barrier(tuple(sent)))
        arrived = {}
        if outer is not None:
            arrived[0] = lax.ppermute(sent[0], "tensor", OUTER)
        if 1 in values:
            arrived[1] = lax.ppermute(sent[-1], "tensor", MIDDLE)
        made = ()
        if slot + 1 < chunks:
            ready = False
            made = into_call(
                starts[slot + 1],
                CHUNKS[slot + 1],
                after(side, *sent),
                spread,
                gathered,
                mains[2] if ready else gate_weight,
                up_weight,
                adapter_lift_in,
                ready,
            )
        done = slot - 6
        if done == 0:
            early = pair(0)
            zero = jnp.zeros((adapter_proj_out.shape[1], gathered.shape[0]), F32)
            ranks, _ = project_call(starts[0], 0, 1, after(side, *sent), slot_row, early, adapter_proj_out, zero)
            made = (ranks,)
        elif done > 0:
            ranks, ahead = project_call(
                starts[1], starts[2], CHUNKS[2], after(side, *sent), slot_row, pair(1), adapter_proj_out, ranks
            )
            sums = down_call(starts[0], after(side, ranks), early, down_weight, None)
            made = (ranks, ahead, sums)
        *came, = lax.optimization_barrier((*arrived.values(), *made))
        arrived = dict(zip(arrived, came))
        made = came[len(arrived):]
        if slot + 1 < chunks:
            near[slot + 1], far[slot + 1] = made
        elif done == 0:
            (ranks,) = made
        elif done > 0:
            ranks, ahead, sums = made
        for c, stage in live:
            value = arrived[stage % 3 % 2]
            units, width = (2, 1)[stage // 3], CHUNKS[c] * CELL
            hop[c] = value[:units, :, :width]
    ranks = project_last_call(side, slot_row, pair(2), ahead, ranks)
    rank_out, made = sum_everywhere(
        ranks,
        [
            (1, lambda tie: down_call(starts[1], after(side, tie), pair(1), down_weight, sums, adapter_lift_out)),
            (2, lambda tie, before: (down_call(starts[2], after(side, tie), pair(2), down_weight, before[0]), before[1])),
        ],
    )
    return scatter_dp(last_call(slot_dp[None, :], rank_out.astype(BF16), *made[-1]))


def solution(mesh):
    on_line = mesh.shape["tensor"] == 4 and mesh.shape["dp"] == 8
    placed = (
        P("dp", "tensor"),
        P("tensor", "dp"),
        P("tensor", "dp"),
        P("dp", "tensor"),
        P("dp", None, "tensor"),
        P("tensor", None, None, "dp"),
        P("tensor", None, "dp"),
        P("dp", None, "tensor"),
        P(),
        P(),
        P(),
    )
    return jax.shard_map(
        line_device if on_line else general_device, mesh=mesh, in_specs=placed, out_specs=P("dp", "tensor"), check_vma=False
    )
```

```python
import functools

import jax
import jax.numpy as jnp
from jax import lax
from jax.experimental import pallas as pl
from jax.experimental.pallas import tpu as pltpu
from jax.sharding import PartitionSpec as P

CELL = 256
CHUNKS = (4, 5, 5)
VMEM_LIMIT = 40 << 20
COST = pl.CostEstimate(flops=8000000000, bytes_accessed=30000000, transcendentals=0)
F32 = jnp.float32
BF16 = jnp.bfloat16


def lookup(keys, table):
    hits = keys[:, None] == jnp.arange(table.shape[0], dtype=jnp.int32)[None, :]
    return jnp.sum(jnp.where(hits, table[None, :], 0), axis=1)


def owned(slot_of, first_slot, amount):
    places = first_slot + jnp.arange(amount, dtype=jnp.int32)
    return (slot_of[:, None] == places[None, :]).astype(jnp.bfloat16)


def general_device(
    tokens,
    gate_weight,
    up_weight,
    down_weight,
    adapter_proj_in,
    adapter_lift_in,
    adapter_proj_out,
    adapter_lift_out,
    token_request,
    request_adapter,
    adapter_slot,
):
    slot_of = lookup(lookup(token_request, request_adapter), adapter_slot)
    dp_index = lax.axis_index("dp")
    tensor_index = lax.axis_index("tensor")
    per_dp = adapter_proj_in.shape[0]
    per_tensor = adapter_lift_in.shape[0]
    rank = adapter_lift_out.shape[1]
    gathered = lax.all_gather(tokens, "dp", axis=0, tiled=True)
    total_rows = gathered.shape[0]
    mask_store_dp = owned(slot_of, dp_index * per_dp, per_dp)
    mask_store_tensor = owned(slot_of, tensor_index * per_tensor, per_tensor)
    projected = jnp.einsum(
        "td,srd->tsr", gathered, adapter_proj_in, preferred_element_type=jnp.float32
    )
    rank_part = jnp.sum(projected * mask_store_dp.astype(jnp.float32)[:, :, None], axis=1)
    rank_in = lax.psum(rank_part, ("dp", "tensor")).astype(jnp.bfloat16)
    rank_in = rank_in.reshape(total_rows, 2, rank)
    spread = rank_in[:, None, :, :] * mask_store_tensor[:, :, None, None]
    adapt_in = jnp.einsum(
        "tscr,scrf->tcf", spread, adapter_lift_in, preferred_element_type=jnp.float32
    )
    row_block = gathered
    gate_part = jnp.dot(row_block, gate_weight, preferred_element_type=jnp.float32)
    up_part = jnp.dot(row_block, up_weight, preferred_element_type=jnp.float32)
    extra = adapt_in
    shares = lax.psum_scatter(
        (jnp.stack([gate_part, up_part], axis=1) + extra).astype(jnp.bfloat16),
        "tensor",
        scatter_dimension=0,
        tiled=True,
    ).astype(jnp.float32)
    hidden = (jax.nn.silu(shares[:, 0]) * shares[:, 1]).astype(jnp.bfloat16)
    hidden_all = lax.all_gather(hidden, "tensor", axis=0, tiled=True)
    projected_out = jnp.einsum(
        "tf,srf->tsr", hidden_all, adapter_proj_out, preferred_element_type=jnp.float32
    )
    rank_part_out = jnp.sum(
        projected_out * mask_store_tensor.astype(jnp.float32)[:, :, None], axis=1
    )
    rank_out = lax.psum(rank_part_out, ("dp", "tensor")).astype(jnp.bfloat16)
    spread_out = rank_out[:, None, :] * mask_store_dp[:, :, None]
    adapt_out = jnp.einsum(
        "tsr,srd->td", spread_out, adapter_lift_out, preferred_element_type=jnp.float32
    )
    row_block = hidden_all
    extra = adapt_out
    return lax.psum_scatter(
        (jnp.dot(row_block, down_weight, preferred_element_type=jnp.float32) + extra).astype(
            jnp.bfloat16
        ),
        "dp",
        scatter_dimension=0,
        tiled=True,
    )


OUTER = [(0, 1), (1, 0), (2, 3), (3, 2)]
MIDDLE = [(1, 2), (2, 1)]


def masked_project(block, rows, slot_row, first):
    slots, rank, depth = block.shape
    full = lax.dot_general(
        block.reshape(slots * rank, depth), rows, (((1,), (1,)), ((), ())), preferred_element_type=F32
    ).reshape(slots, rank, rows.shape[0])
    ids = first + lax.broadcasted_iota(jnp.int32, full.shape, 0)
    return jnp.sum(jnp.where(ids == slot_row[None], full, 0.0), axis=0)


def spread_rows(rank_t, slot_row, slots):
    rank, total = rank_t.shape
    width = slots * rank
    slot_col = jnp.broadcast_to(slot_row.astype(F32), (8, total)).T[:, :1].astype(jnp.int32)
    lane = lax.broadcasted_iota(jnp.int32, (rank, width), 1)
    row = lax.broadcasted_iota(jnp.int32, (rank, width), 0)
    copies = (lax.rem(lane, rank) == row).astype(F32).astype(BF16)
    tiled = lax.dot_general(
        rank_t.astype(F32).T.astype(BF16), copies, (((1,), (0,)), ((), ())), preferred_element_type=F32
    )
    owner = lax.div(lax.broadcasted_iota(jnp.int32, tiled.shape, 1), rank)
    return jnp.where(owner == slot_col, tiled, 0.0).astype(BF16)


IN_VMEM = pl.BlockSpec(memory_space=pltpu.VMEM)
IN_SMEM = pl.BlockSpec(memory_space=pltpu.SMEM)
ANYWHERE = pl.BlockSpec(memory_space=pl.ANY)
ROWS = 512
GROUP = 16


def call(kernel, name, in_specs, outs, scratch):
    return pl.pallas_call(
        kernel,
        in_specs=in_specs,
        out_specs=jax.tree.map(lambda _: IN_VMEM, outs),
        out_shape=outs,
        scratch_shapes=scratch,
        compiler_params=pltpu.CompilerParams(vmem_limit_bytes=VMEM_LIMIT),
        cost_estimate=COST,
        name=name,
    )


def fetch(parts, sems):
    copies = [pltpu.make_async_copy(src, dst, sems.at[at]) for at, (src, dst) in enumerate(parts)]
    for copy in copies:
        copy.start()
    return copies


def rank_in_kernel(slot_ref, rows_ref, proj_ref, out_ref):
    out_ref[...] = masked_project(proj_ref[...], rows_ref[...], slot_ref[...], 0)


def rank_in_call(slot_row, rows, proj):
    outs = jax.ShapeDtypeStruct((proj.shape[1], rows.shape[0]), F32)
    return call(rank_in_kernel, "rank_in", [IN_VMEM] * 3, outs, [])(slot_row, rows, proj)


def half_rows(side, which, half):
    start = side * half if which == 0 else (1 - side) * half
    return pl.ds(pl.multiple_of(start, 16), half)


def weight_parts(weight_ref, held_ref, first):
    blocks, rows, width = held_ref.shape
    return [
        (weight_ref.at[pl.ds(k * rows, rows), pl.ds(first * CELL, width)], held_ref.at[k]) for k in range(blocks)
    ]


def lift_parts(lift_ref, held_ref, first):
    groups, slots = held_ref.shape[:2]
    width = held_ref.shape[-1]
    return [
        (lift_ref.at[pl.ds(g * slots, slots), :, :, pl.ds(first * CELL, width)], held_ref.at[g])
        for g in range(groups)
    ]


def add_product(total_ref, fresh, left, right):
    product = jnp.dot(left, right, preferred_element_type=F32)
    total_ref[...] = product if fresh else total_ref[...] + product


def add_lift(total_ref, spread_ref, held_ref, g):
    _, slots, _, rank, width = held_ref.shape
    depth = slots * rank
    for c in range(2):
        left = spread_ref[c, :, g * depth:(g + 1) * depth]
        add_product(total_ref.at[c], False, left, held_ref[g, :, c].reshape(depth, width))


def halves_out(total_ref, side, near_ref, far_ref):
    half = near_ref.shape[1]
    for c in range(2):
        near_ref[c] = total_ref[c, half_rows(side, 0, half), :].astype(BF16)
        far_ref[c] = total_ref[c, half_rows(side, 1, half), :].astype(BF16)


def main_kernel(first, rows_ref, weight_ref, out_ref, held_ref, sems):
    copies = fetch(weight_parts(weight_ref, held_ref, first), sems)
    for k, copy in enumerate(copies):
        copy.wait()
        add_product(out_ref, k == 0, rows_ref[:, k * ROWS:(k + 1) * ROWS], held_ref[k])


def main_call(first, cells, rows, weight):
    total, depth = rows.shape
    blocks, width = depth // ROWS, cells * CELL
    return call(
        functools.partial(main_kernel, first),
        "main",
        [IN_VMEM, ANYWHERE],
        jax.ShapeDtypeStruct((total, width), F32),
        [pltpu.VMEM((blocks, ROWS, width), BF16), pltpu.SemaphoreType.DMA((blocks,))],
    )(rows, weight)


def first_kernel(side_ref, slot_ref, rank_ref, gate_ref, up_ref, lift_ref, near_ref, far_ref, spread_ref, total_ref, held_ref, sems):
    copies = fetch(lift_parts(lift_ref, held_ref, 0), sems)
    slots, _, rank, _ = lift_ref.shape
    for c, main_ref in ((0, gate_ref), (1, up_ref)):
        spread_ref[c] = spread_rows(rank_ref[c * rank:(c + 1) * rank, :], slot_ref[...], slots)
        total_ref[c] = main_ref[...]
    for g, copy in enumerate(copies):
        copy.wait()
        add_lift(total_ref, spread_ref, held_ref, g)
    halves_out(total_ref, side_ref[0], near_ref, far_ref)


def lift_held(lift, width):
    slots, two, rank, _ = lift.shape
    return pltpu.VMEM((slots // GROUP, GROUP, two, rank, width), BF16)


def first_call(side, slot_row, rank_t, gate, up, lift):
    slots, _, rank, _ = lift.shape
    total, width = gate.shape
    piece = jax.ShapeDtypeStruct((2, total // 2, width), BF16)
    return call(
        first_kernel,
        "first",
        [IN_SMEM] + [IN_VMEM] * 4 + [ANYWHERE],
        [piece, piece, jax.ShapeDtypeStruct((2, total, slots * rank), BF16)],
        [pltpu.VMEM((2, total, width), F32), lift_held(lift, width), pltpu.SemaphoreType.DMA((slots // GROUP,))],
    )(side, slot_row, rank_t, gate, up, lift)


def into_kernel(first, ready, side_ref, rows_ref, spread_ref, gate_ref, up_ref, lift_ref, near_ref, far_ref, total_ref, held_ref, lift_buf, sems):
    gates = [(gate_ref, total_ref.at[0])] if ready else weight_parts(gate_ref, held_ref.at[1], first)
    ups = weight_parts(up_ref, held_ref.at[0], first)
    lifts = lift_parts(lift_ref, lift_buf, first)
    copies = fetch(gates + ups + lifts, sems)
    at = 0
    for c, count in ((0, len(gates)), (1, len(ups))):
        for k in range(count):
            copies[at].wait()
            at += 1
            if c == 1 or not ready:
                add_product(total_ref.at[c], k == 0, rows_ref[:, k * ROWS:(k + 1) * ROWS], held_ref[1 - c, k])
    for g, copy in enumerate(copies[at:]):
        copy.wait()
        add_lift(total_ref, spread_ref, lift_buf, g)
    halves_out(total_ref, side_ref[0], near_ref, far_ref)


def into_call(first, cells, side, spread, rows, gate, up_weight, lift, ready):
    total, depth = rows.shape
    blocks, width = depth // ROWS, cells * CELL
    copies = (1 if ready else blocks) + blocks + lift.shape[0] // GROUP
    return call(
        functools.partial(into_kernel, first, ready),
        "into",
        [IN_SMEM, IN_VMEM, IN_VMEM] + [ANYWHERE] * 3,
        [jax.ShapeDtypeStruct((2, total // 2, width), BF16)] * 2,
        [
            pltpu.VMEM((2, total, width), F32),
            pltpu.VMEM((1 if ready else 2, blocks, ROWS, width), BF16),
            lift_held(lift, width),
            pltpu.SemaphoreType.DMA((copies,)),
        ],
    )(side, rows, spread, gate, up_weight, lift)


def whole_hidden(side, near_ref, far_ref, hidden_ref):
    half = near_ref.shape[0]
    hidden_ref[half_rows(side, 0, half), :] = near_ref[...]
    hidden_ref[half_rows(side, 1, half), :] = far_ref[...]


def project_parts(proj_ref, held_ref, first):
    groups, slots = held_ref.shape[:2]
    columns = pl.ds(first * CELL, held_ref.shape[-1])
    return [(proj_ref.at[pl.ds(g * slots, slots), :, columns], held_ref.at[g]) for g in range(groups)]


def project_kernel(first, later, side_ref, slot_ref, near_ref, far_ref, proj_ref, before_ref, out_ref, brought_ref, hidden_ref, held_ref, sems):
    parts = project_parts(proj_ref, held_ref, first)
    copies = fetch(parts + project_parts(proj_ref, brought_ref, later) * (later > 0), sems)
    whole_hidden(side_ref[0], near_ref, far_ref, hidden_ref)
    total = before_ref[...]
    slots = held_ref.shape[1]
    for g in range(len(parts)):
        copies[g].wait()
        total += masked_project(held_ref[g], hidden_ref[...], slot_ref[...], g * slots)
    out_ref[...] = total
    for copy in copies[len(parts):]:
        copy.wait()


def project_call(first, later, later_cells, side, slot_row, parts, proj, carried):
    slots, rank, _ = proj.shape
    half, width = parts[0].shape
    groups = slots // GROUP
    held = (groups, GROUP, rank)
    return call(
        functools.partial(project_kernel, first, later),
        "project",
        [IN_SMEM] + [IN_VMEM] * 3 + [ANYWHERE, IN_VMEM],
        [
            jax.ShapeDtypeStruct((rank, 2 * half), F32),
            jax.ShapeDtypeStruct((*held, later_cells * CELL), BF16),
        ],
        [
            pltpu.VMEM((2 * half, width), BF16),
            pltpu.VMEM((*held, width), BF16),
            pltpu.SemaphoreType.DMA((2 * groups,)),
        ],
    )(side, slot_row, *parts, proj, carried)


def project_last_kernel(side_ref, slot_ref, near_ref, far_ref, held_ref, before_ref, out_ref, hidden_ref):
    whole_hidden(side_ref[0], near_ref, far_ref, hidden_ref)
    total = before_ref[...]
    slots = held_ref.shape[1]
    for g in range(held_ref.shape[0]):
        total += masked_project(held_ref[g], hidden_ref[...], slot_ref[...], g * slots)
    out_ref[...] = total


def project_last_call(side, slot_row, parts, held, carried):
    half, width = parts[0].shape
    return call(
        project_last_kernel,
        "project",
        [IN_SMEM] + [IN_VMEM] * 5,
        jax.ShapeDtypeStruct(carried.shape, F32),
        [pltpu.VMEM((2 * half, width), BF16)],
    )(side, slot_row, *parts, held, carried)


def down_kernel(first, bring, side_ref, near_ref, far_ref, down_ref, *rest):
    rest, (hidden_ref, held_ref, sems) = rest[:-3], rest[-3:]
    if bring:
        rest, (later_ref, out_ref, brought_ref) = rest[:-3], rest[-3:]
    else:
        rest, out_ref = rest[:-1], rest[-1]
    cells = held_ref.shape[0]
    parts = [(down_ref.at[pl.ds((first + k) * CELL, CELL), :], held_ref.at[k]) for k in range(cells)]
    if bring:
        parts.append((later_ref, brought_ref))
    copies = fetch(parts, sems)
    whole_hidden(side_ref[0], near_ref, far_ref, hidden_ref)
    for k in range(cells):
        copies[k].wait()
        product = jnp.dot(hidden_ref[:, k * CELL:(k + 1) * CELL], held_ref[k], preferred_element_type=F32)
        if k > 0:
            product += out_ref[...]
        elif rest:
            product += rest[0][...]
        out_ref[...] = product
    if bring:
        copies[cells].wait()


def down_call(first, side, parts, down, carried, later=None):
    half, width = parts[0].shape
    out = down.shape[1]
    cells = width // CELL
    extra = () if carried is None else (carried,)
    bring = () if later is None else (later,)
    sums = jax.ShapeDtypeStruct((2 * half, out), F32)
    return call(
        functools.partial(down_kernel, first, len(bring)),
        "down",
        [IN_SMEM, IN_VMEM, IN_VMEM, ANYWHERE] + [IN_VMEM for _ in extra] + [ANYWHERE for _ in bring],
        [sums, jax.ShapeDtypeStruct(later.shape, later.dtype)] if bring else sums,
        [
            pltpu.VMEM((2 * half, width), BF16),
            pltpu.VMEM((cells, CELL, out), BF16),
            pltpu.SemaphoreType.DMA((cells + len(bring),)),
        ],
    )(side, *parts, down, *extra, *bring)


def last_kernel(slot_ref, rank_ref, sum_ref, lift_ref, out_ref):
    slots, rank, width = lift_ref.shape
    spread = spread_rows(rank_ref[...], slot_ref[...], slots)
    extra = jnp.dot(spread, lift_ref[...].reshape(slots * rank, width), preferred_element_type=F32)
    out_ref[...] = (sum_ref[...] + extra).astype(BF16)


def last_call(slot_row, rank_t, sums, lift):
    return call(
        last_kernel, "last", [IN_VMEM] * 4, jax.ShapeDtypeStruct(sums.shape, BF16), []
    )(slot_row, rank_t, sums, lift)


def after(value, *behind):
    return lax.optimization_barrier((value, *behind))[0]


def swap(value, axis, size, mask):
    return lax.ppermute(value, axis, [(i, i ^ mask) for i in range(size)])


def gather_dp(block, beside):
    me = lax.axis_index("dp")
    chip = me >> 1
    near = jnp.stack([block] + [swap(block, "dp", 8, 2 * mask) for mask in (1, 2, 3)])
    near, beside = lax.optimization_barrier((near, beside))
    other = swap(near, "dp", 8, 1)
    both = jnp.where((me & 1) == 0, jnp.stack([near, other], 1), jnp.stack([other, near], 1))
    both = jnp.where((chip & 1) == 0, both, jnp.stack([both[1], both[0], both[3], both[2]]))
    both = jnp.where((chip & 2) == 0, both, jnp.stack([both[2], both[3], both[0], both[1]]))
    return both.reshape(8 * block.shape[0], block.shape[1]), beside


def sum_everywhere(value, beside=()):
    made = []
    for stage, (axis, size, masks) in enumerate(
        (("dp", 8, (1,)), ("dp", 8, (6, 2, 4)), ("tensor", 4, (1,)), ("tensor", 4, (2,)))
    ):
        others = [swap(value, axis, size, mask) for mask in masks]
        for when, work in beside:
            if when == stage:
                made.append(work(value, *made[-1:]))
                others, made[-1] = lax.optimization_barrier((others, made[-1]))
        value = sum(others, value)
    return value, made


def scatter_dp(rows):
    total, width = rows.shape
    me = lax.axis_index("dp")
    core = me & 1
    blocks = rows.reshape(4, 2, total // 8, width)
    mine = lax.dynamic_index_in_dim(blocks, core, 1, keepdims=False)
    other = lax.dynamic_index_in_dim(blocks, 1 - core, 1, keepdims=False)
    both = (mine.astype(F32) + swap(other, "dp", 8, 1).astype(F32)).astype(BF16)
    chip = me >> 1
    kept = lax.dynamic_index_in_dim(both, chip, 0, keepdims=False).astype(F32)
    for mask in (3, 1, 2):
        sent = lax.dynamic_index_in_dim(both, chip ^ mask, 0, keepdims=False)
        kept = kept + swap(sent, "dp", 8, 2 * mask).astype(F32)
    return kept.astype(BF16)


def line_device(
    tokens,
    gate_weight,
    up_weight,
    down_weight,
    adapter_proj_in,
    adapter_lift_in,
    adapter_proj_out,
    adapter_lift_out,
    token_request,
    request_adapter,
    adapter_slot,
):
    slot_of = lookup(lookup(token_request, request_adapter), adapter_slot)
    gathered, slot_of = gather_dp(tokens, slot_of)
    dp_index = lax.axis_index("dp")
    tensor_index = lax.axis_index("tensor")
    side = (tensor_index >> 1).astype(jnp.int32).reshape(1)
    is_end = (tensor_index == 0) | (tensor_index == 3)
    slot_dp = slot_of - dp_index * adapter_proj_in.shape[0]
    slot_tensor = slot_of - tensor_index * adapter_lift_in.shape[0]
    rank_part = rank_in_call(slot_dp[None, :], gathered, adapter_proj_in)
    rank_in, mains = sum_everywhere(
        rank_part,
        [
            (1, lambda tie: main_call(0, CHUNKS[0], after(gathered, tie), gate_weight)),
            (2, lambda tie, before: main_call(0, CHUNKS[0], after(gathered, tie, before), up_weight)),
        ],
    )
    rank_in = rank_in.astype(BF16)
    slot_row = slot_tensor[None, :]
    chunks = len(CHUNKS)
    starts = [sum(CHUNKS[:c]) for c in range(chunks)]
    near, far, hop, hidden_near, hidden_far = ({} for _ in range(5))

    def operand(c, stage):
        if stage == 0:
            return far[c]
        if stage == 1:
            return (far[c].astype(F32) + hop[c].astype(F32)).astype(BF16)
        if stage == 2:
            return (near[c].astype(F32) + hop[c].astype(F32)).astype(BF16)
        if stage == 3:
            both = near[c].astype(F32) + hop[c].astype(F32)
            hidden_near[c] = (jax.nn.silu(both[0]) * both[1]).astype(BF16)[None]
            return hidden_near[c]
        if stage == 4:
            hidden_near[c] = jnp.where(is_end, hidden_near[c], hop[c])
            return hop[c]
        hidden_far[c] = hop[c]
        return hop[c]

    def pair(c):
        return [hidden_near[c][0], jnp.where(is_end, hop[c], hidden_far[c])[0]]

    def padded(value, shape):
        return jnp.pad(value, [(0, b - a) for a, b in zip(value.shape, shape)])

    near[0], far[0], spread = first_call(side, slot_row, rank_in, *mains[:2], adapter_lift_in)
    sums, ranks = None, None
    for slot in range(chunks + 5):
        live = [(slot - stage, stage) for stage in range(6) if 0 <= slot - stage < chunks]
        values = {stage % 3: operand(c, stage) for c, stage in live}
        if 0 in values and 2 in values:
            shape = tuple(max(a, b) for a, b in zip(values[0].shape, values[2].shape))
            outer = jnp.where(is_end, padded(values[0], shape), padded(values[2], shape))
        else:
            outer = values.get(0, values.get(2))
        sent = [value for value in (outer, values.get(1)) if value is not None]
        sent = list(lax.optimization_barrier(tuple(sent)))
        arrived = {}
        if outer is not None:
            arrived[0] = lax.ppermute(sent[0], "tensor", OUTER)
        if 1 in values:
            arrived[1] = lax.ppermute(sent[-1], "tensor", MIDDLE)
        made = ()
        if slot + 1 < chunks:
            ready = False
            made = into_call(
                starts[slot + 1],
                CHUNKS[slot + 1],
                after(side, *sent),
                spread,
                gathered,
                mains[2] if ready else gate_weight,
                up_weight,
                adapter_lift_in,
                ready,
            )
        done = slot - 6
        if done == 0:
            early = pair(0)
            zero = jnp.zeros((adapter_proj_out.shape[1], gathered.shape[0]), F32)
            ranks, _ = project_call(starts[0], 0, 1, after(side, *sent), slot_row, early, adapter_proj_out, zero)
            made = (ranks,)
        elif done > 0:
            ranks, ahead = project_call(
                starts[1], starts[2], CHUNKS[2], after(side, *sent), slot_row, pair(1), adapter_proj_out, ranks
            )
            sums = down_call(starts[0], after(side, ranks), early, down_weight, None)
            made = (ranks, ahead, sums)
        *came, = lax.optimization_barrier((*arrived.values(), *made))
        arrived = dict(zip(arrived, came))
        made = came[len(arrived):]
        if slot + 1 < chunks:
            near[slot + 1], far[slot + 1] = made
        elif done == 0:
            (ranks,) = made
        elif done > 0:
            ranks, ahead, sums = made
        for c, stage in live:
            value = arrived[stage % 3 % 2]
            units, width = (2, 1)[stage // 3], CHUNKS[c] * CELL
            hop[c] = value[:units, :, :width]
    ranks = project_last_call(side, slot_row, pair(2), ahead, ranks)
    rank_out, made = sum_everywhere(
        ranks,
        [
            (2, lambda tie: down_call(starts[1], after(side, tie), pair(1), down_weight, sums)),
            (3, lambda tie, before: down_call(starts[2], after(side, tie), pair(2), down_weight, before)),
        ],
    )
    return scatter_dp(last_call(slot_dp[None, :], rank_out.astype(BF16), made[-1], adapter_lift_out))


def solution(mesh):
    on_line = mesh.shape["tensor"] == 4 and mesh.shape["dp"] == 8
    placed = (
        P("dp", "tensor"),
        P("tensor", "dp"),
        P("tensor", "dp"),
        P("dp", "tensor"),
        P("dp", None, "tensor"),
        P("tensor", None, None, "dp"),
        P("tensor", None, "dp"),
        P("dp", None, "tensor"),
        P(),
        P(),
        P(),
    )
    return jax.shard_map(
        line_device if on_line else general_device, mesh=mesh, in_specs=placed, out_specs=P("dp", "tensor"), check_vma=False
    )
```

```python
import functools

import jax
import jax.numpy as jnp
from jax import lax
from jax.experimental import pallas as pl
from jax.experimental.pallas import tpu as pltpu
from jax.sharding import PartitionSpec as P

CELL = 256
CHUNKS = (4, 5, 5)
VMEM_LIMIT = 40 << 20
COST = pl.CostEstimate(flops=8000000000, bytes_accessed=30000000, transcendentals=0)
F32 = jnp.float32
BF16 = jnp.bfloat16


def lookup(keys, table):
    hits = keys[:, None] == jnp.arange(table.shape[0], dtype=jnp.int32)[None, :]
    return jnp.sum(jnp.where(hits, table[None, :], 0), axis=1)


def owned(slot_of, first_slot, amount):
    places = first_slot + jnp.arange(amount, dtype=jnp.int32)
    return (slot_of[:, None] == places[None, :]).astype(jnp.bfloat16)


def general_device(
    tokens,
    gate_weight,
    up_weight,
    down_weight,
    adapter_proj_in,
    adapter_lift_in,
    adapter_proj_out,
    adapter_lift_out,
    token_request,
    request_adapter,
    adapter_slot,
):
    slot_of = lookup(lookup(token_request, request_adapter), adapter_slot)
    dp_index = lax.axis_index("dp")
    tensor_index = lax.axis_index("tensor")
    per_dp = adapter_proj_in.shape[0]
    per_tensor = adapter_lift_in.shape[0]
    rank = adapter_lift_out.shape[1]
    gathered = lax.all_gather(tokens, "dp", axis=0, tiled=True)
    total_rows = gathered.shape[0]
    mask_store_dp = owned(slot_of, dp_index * per_dp, per_dp)
    mask_store_tensor = owned(slot_of, tensor_index * per_tensor, per_tensor)
    projected = jnp.einsum(
        "td,srd->tsr", gathered, adapter_proj_in, preferred_element_type=jnp.float32
    )
    rank_part = jnp.sum(projected * mask_store_dp.astype(jnp.float32)[:, :, None], axis=1)
    rank_in = lax.psum(rank_part, ("dp", "tensor")).astype(jnp.bfloat16)
    rank_in = rank_in.reshape(total_rows, 2, rank)
    spread = rank_in[:, None, :, :] * mask_store_tensor[:, :, None, None]
    adapt_in = jnp.einsum(
        "tscr,scrf->tcf", spread, adapter_lift_in, preferred_element_type=jnp.float32
    )
    row_block = gathered
    gate_part = jnp.dot(row_block, gate_weight, preferred_element_type=jnp.float32)
    up_part = jnp.dot(row_block, up_weight, preferred_element_type=jnp.float32)
    extra = adapt_in
    shares = lax.psum_scatter(
        (jnp.stack([gate_part, up_part], axis=1) + extra).astype(jnp.bfloat16),
        "tensor",
        scatter_dimension=0,
        tiled=True,
    ).astype(jnp.float32)
    hidden = (jax.nn.silu(shares[:, 0]) * shares[:, 1]).astype(jnp.bfloat16)
    hidden_all = lax.all_gather(hidden, "tensor", axis=0, tiled=True)
    projected_out = jnp.einsum(
        "tf,srf->tsr", hidden_all, adapter_proj_out, preferred_element_type=jnp.float32
    )
    rank_part_out = jnp.sum(
        projected_out * mask_store_tensor.astype(jnp.float32)[:, :, None], axis=1
    )
    rank_out = lax.psum(rank_part_out, ("dp", "tensor")).astype(jnp.bfloat16)
    spread_out = rank_out[:, None, :] * mask_store_dp[:, :, None]
    adapt_out = jnp.einsum(
        "tsr,srd->td", spread_out, adapter_lift_out, preferred_element_type=jnp.float32
    )
    row_block = hidden_all
    extra = adapt_out
    return lax.psum_scatter(
        (jnp.dot(row_block, down_weight, preferred_element_type=jnp.float32) + extra).astype(
            jnp.bfloat16
        ),
        "dp",
        scatter_dimension=0,
        tiled=True,
    )


OUTER = [(0, 1), (1, 0), (2, 3), (3, 2)]
MIDDLE = [(1, 2), (2, 1)]


def masked_project(block, rows, slot_row, first):
    slots, rank, depth = block.shape
    full = lax.dot_general(
        block.reshape(slots * rank, depth), rows, (((1,), (1,)), ((), ())), preferred_element_type=F32
    ).reshape(slots, rank, rows.shape[0])
    ids = first + lax.broadcasted_iota(jnp.int32, full.shape, 0)
    return jnp.sum(jnp.where(ids == slot_row[None], full, 0.0), axis=0)


def spread_rows(rank_t, slot_row, slots):
    rank, total = rank_t.shape
    width = slots * rank
    slot_col = jnp.broadcast_to(slot_row.astype(F32), (8, total)).T[:, :1].astype(jnp.int32)
    lane = lax.broadcasted_iota(jnp.int32, (rank, width), 1)
    row = lax.broadcasted_iota(jnp.int32, (rank, width), 0)
    copies = (lax.rem(lane, rank) == row).astype(F32).astype(BF16)
    tiled = lax.dot_general(
        rank_t.astype(F32).T.astype(BF16), copies, (((1,), (0,)), ((), ())), preferred_element_type=F32
    )
    owner = lax.div(lax.broadcasted_iota(jnp.int32, tiled.shape, 1), rank)
    return jnp.where(owner == slot_col, tiled, 0.0).astype(BF16)


IN_VMEM = pl.BlockSpec(memory_space=pltpu.VMEM)
IN_SMEM = pl.BlockSpec(memory_space=pltpu.SMEM)
ANYWHERE = pl.BlockSpec(memory_space=pl.ANY)
ROWS = 512
GROUP = 16


def call(kernel, name, in_specs, outs, scratch):
    return pl.pallas_call(
        kernel,
        in_specs=in_specs,
        out_specs=jax.tree.map(lambda _: IN_VMEM, outs),
        out_shape=outs,
        scratch_shapes=scratch,
        compiler_params=pltpu.CompilerParams(vmem_limit_bytes=VMEM_LIMIT),
        cost_estimate=COST,
        name=name,
    )


def fetch(parts, sems):
    copies = [pltpu.make_async_copy(src, dst, sems.at[at]) for at, (src, dst) in enumerate(parts)]
    for copy in copies:
        copy.start()
    return copies


def rank_in_kernel(slot_ref, rows_ref, proj_ref, out_ref):
    out_ref[...] = masked_project(proj_ref[...], rows_ref[...], slot_ref[...], 0)


def rank_in_call(slot_row, rows, proj):
    outs = jax.ShapeDtypeStruct((proj.shape[1], rows.shape[0]), F32)
    return call(rank_in_kernel, "rank_in", [IN_VMEM] * 3, outs, [])(slot_row, rows, proj)


def half_rows(side, which, half):
    start = side * half if which == 0 else (1 - side) * half
    return pl.ds(pl.multiple_of(start, 16), half)


def weight_parts(weight_ref, held_ref, first):
    blocks, rows, width = held_ref.shape
    return [
        (weight_ref.at[pl.ds(k * rows, rows), pl.ds(first * CELL, width)], held_ref.at[k]) for k in range(blocks)
    ]


def lift_parts(lift_ref, held_ref, first):
    groups, slots = held_ref.shape[:2]
    width = held_ref.shape[-1]
    return [
        (lift_ref.at[pl.ds(g * slots, slots), :, :, pl.ds(first * CELL, width)], held_ref.at[g])
        for g in range(groups)
    ]


def add_product(total_ref, fresh, left, right):
    product = jnp.dot(left, right, preferred_element_type=F32)
    total_ref[...] = product if fresh else total_ref[...] + product


def add_lift(total_ref, spread_ref, held_ref, g):
    _, slots, _, rank, width = held_ref.shape
    depth = slots * rank
    for c in range(2):
        left = spread_ref[c, :, g * depth:(g + 1) * depth]
        add_product(total_ref.at[c], False, left, held_ref[g, :, c].reshape(depth, width))


def halves_out(total_ref, side, near_ref, far_ref):
    half = near_ref.shape[1]
    for c in range(2):
        near_ref[c] = total_ref[c, half_rows(side, 0, half), :].astype(BF16)
        far_ref[c] = total_ref[c, half_rows(side, 1, half), :].astype(BF16)


def main_kernel(first, rows_ref, weight_ref, out_ref, held_ref, sems):
    copies = fetch(weight_parts(weight_ref, held_ref, first), sems)
    for k, copy in enumerate(copies):
        copy.wait()
        add_product(out_ref, k == 0, rows_ref[:, k * ROWS:(k + 1) * ROWS], held_ref[k])


def main_call(first, cells, rows, weight):
    total, depth = rows.shape
    blocks, width = depth // ROWS, cells * CELL
    return call(
        functools.partial(main_kernel, first),
        "main",
        [IN_VMEM, ANYWHERE],
        jax.ShapeDtypeStruct((total, width), F32),
        [pltpu.VMEM((blocks, ROWS, width), BF16), pltpu.SemaphoreType.DMA((blocks,))],
    )(rows, weight)


def first_kernel(side_ref, slot_ref, rank_ref, gate_ref, up_ref, lift_ref, near_ref, far_ref, spread_ref, total_ref, held_ref, sems):
    copies = fetch(lift_parts(lift_ref, held_ref, 0), sems)
    slots, _, rank, _ = lift_ref.shape
    for c, main_ref in ((0, gate_ref), (1, up_ref)):
        spread_ref[c] = spread_rows(rank_ref[c * rank:(c + 1) * rank, :], slot_ref[...], slots)
        total_ref[c] = main_ref[...]
    for g, copy in enumerate(copies):
        copy.wait()
        add_lift(total_ref, spread_ref, held_ref, g)
    halves_out(total_ref, side_ref[0], near_ref, far_ref)


def lift_held(lift, width):
    slots, two, rank, _ = lift.shape
    return pltpu.VMEM((slots // GROUP, GROUP, two, rank, width), BF16)


def first_call(side, slot_row, rank_t, gate, up, lift):
    slots, _, rank, _ = lift.shape
    total, width = gate.shape
    piece = jax.ShapeDtypeStruct((2, total // 2, width), BF16)
    return call(
        first_kernel,
        "first",
        [IN_SMEM] + [IN_VMEM] * 4 + [ANYWHERE],
        [piece, piece, jax.ShapeDtypeStruct((2, total, slots * rank), BF16)],
        [pltpu.VMEM((2, total, width), F32), lift_held(lift, width), pltpu.SemaphoreType.DMA((slots // GROUP,))],
    )(side, slot_row, rank_t, gate, up, lift)


def into_kernel(first, ready, side_ref, rows_ref, spread_ref, gate_ref, up_ref, lift_ref, near_ref, far_ref, total_ref, held_ref, lift_buf, sems):
    gates = [(gate_ref, total_ref.at[0])] if ready else weight_parts(gate_ref, held_ref.at[1], first)
    ups = weight_parts(up_ref, held_ref.at[0], first)
    lifts = lift_parts(lift_ref, lift_buf, first)
    copies = fetch(gates + ups + lifts, sems)
    at = 0
    for c, count in ((0, len(gates)), (1, len(ups))):
        for k in range(count):
            copies[at].wait()
            at += 1
            if c == 1 or not ready:
                add_product(total_ref.at[c], k == 0, rows_ref[:, k * ROWS:(k + 1) * ROWS], held_ref[1 - c, k])
    for g, copy in enumerate(copies[at:]):
        copy.wait()
        add_lift(total_ref, spread_ref, lift_buf, g)
    halves_out(total_ref, side_ref[0], near_ref, far_ref)


def into_call(first, cells, side, spread, rows, gate, up_weight, lift, ready):
    total, depth = rows.shape
    blocks, width = depth // ROWS, cells * CELL
    copies = (1 if ready else blocks) + blocks + lift.shape[0] // GROUP
    return call(
        functools.partial(into_kernel, first, ready),
        "into",
        [IN_SMEM, IN_VMEM, IN_VMEM] + [ANYWHERE] * 3,
        [jax.ShapeDtypeStruct((2, total // 2, width), BF16)] * 2,
        [
            pltpu.VMEM((2, total, width), F32),
            pltpu.VMEM((1 if ready else 2, blocks, ROWS, width), BF16),
            lift_held(lift, width),
            pltpu.SemaphoreType.DMA((copies,)),
        ],
    )(side, rows, spread, gate, up_weight, lift)


def whole_hidden(side, near_ref, far_ref, hidden_ref):
    half = near_ref.shape[0]
    hidden_ref[half_rows(side, 0, half), :] = near_ref[...]
    hidden_ref[half_rows(side, 1, half), :] = far_ref[...]


def project_parts(proj_ref, held_ref, first):
    groups, slots = held_ref.shape[:2]
    columns = pl.ds(first * CELL, held_ref.shape[-1])
    return [(proj_ref.at[pl.ds(g * slots, slots), :, columns], held_ref.at[g]) for g in range(groups)]


def project_kernel(first, later, side_ref, slot_ref, near_ref, far_ref, proj_ref, before_ref, out_ref, brought_ref, hidden_ref, held_ref, sems):
    parts = project_parts(proj_ref, held_ref, first)
    copies = fetch(parts + project_parts(proj_ref, brought_ref, later) * (later > 0), sems)
    whole_hidden(side_ref[0], near_ref, far_ref, hidden_ref)
    total = before_ref[...]
    slots = held_ref.shape[1]
    for g in range(len(parts)):
        copies[g].wait()
        total += masked_project(held_ref[g], hidden_ref[...], slot_ref[...], g * slots)
    out_ref[...] = total
    for copy in copies[len(parts):]:
        copy.wait()


def project_call(first, later, later_cells, side, slot_row, parts, proj, carried):
    slots, rank, _ = proj.shape
    half, width = parts[0].shape
    groups = slots // GROUP
    held = (groups, GROUP, rank)
    return call(
        functools.partial(project_kernel, first, later),
        "project",
        [IN_SMEM] + [IN_VMEM] * 3 + [ANYWHERE, IN_VMEM],
        [
            jax.ShapeDtypeStruct((rank, 2 * half), F32),
            jax.ShapeDtypeStruct((*held, later_cells * CELL), BF16),
        ],
        [
            pltpu.VMEM((2 * half, width), BF16),
            pltpu.VMEM((*held, width), BF16),
            pltpu.SemaphoreType.DMA((2 * groups,)),
        ],
    )(side, slot_row, *parts, proj, carried)


def project_last_kernel(side_ref, slot_ref, near_ref, far_ref, held_ref, before_ref, out_ref, hidden_ref):
    whole_hidden(side_ref[0], near_ref, far_ref, hidden_ref)
    total = before_ref[...]
    slots = held_ref.shape[1]
    for g in range(held_ref.shape[0]):
        total += masked_project(held_ref[g], hidden_ref[...], slot_ref[...], g * slots)
    out_ref[...] = total


def project_last_call(side, slot_row, parts, held, carried):
    half, width = parts[0].shape
    return call(
        project_last_kernel,
        "project",
        [IN_SMEM] + [IN_VMEM] * 5,
        jax.ShapeDtypeStruct(carried.shape, F32),
        [pltpu.VMEM((2 * half, width), BF16)],
    )(side, slot_row, *parts, held, carried)


def down_kernel(first, bring, side_ref, near_ref, far_ref, down_ref, *rest):
    rest, (hidden_ref, held_ref, sems) = rest[:-3], rest[-3:]
    if bring:
        rest, (later_ref, out_ref, brought_ref) = rest[:-3], rest[-3:]
    else:
        rest, out_ref = rest[:-1], rest[-1]
    cells = held_ref.shape[0]
    parts = [(down_ref.at[pl.ds((first + k) * CELL, CELL), :], held_ref.at[k]) for k in range(cells)]
    if bring:
        parts.append((later_ref, brought_ref))
    copies = fetch(parts, sems)
    whole_hidden(side_ref[0], near_ref, far_ref, hidden_ref)
    for k in range(cells):
        copies[k].wait()
        product = jnp.dot(hidden_ref[:, k * CELL:(k + 1) * CELL], held_ref[k], preferred_element_type=F32)
        if k > 0:
            product += out_ref[...]
        elif rest:
            product += rest[0][...]
        out_ref[...] = product
    if bring:
        copies[cells].wait()


def down_call(first, side, parts, down, carried, later=None):
    half, width = parts[0].shape
    out = down.shape[1]
    cells = width // CELL
    extra = () if carried is None else (carried,)
    bring = () if later is None else (later,)
    sums = jax.ShapeDtypeStruct((2 * half, out), F32)
    return call(
        functools.partial(down_kernel, first, len(bring)),
        "down",
        [IN_SMEM, IN_VMEM, IN_VMEM, ANYWHERE] + [IN_VMEM for _ in extra] + [ANYWHERE for _ in bring],
        [sums, jax.ShapeDtypeStruct(later.shape, later.dtype)] if bring else sums,
        [
            pltpu.VMEM((2 * half, width), BF16),
            pltpu.VMEM((cells, CELL, out), BF16),
            pltpu.SemaphoreType.DMA((cells + len(bring),)),
        ],
    )(side, *parts, down, *extra, *bring)


def last_kernel(slot_ref, rank_ref, sum_ref, lift_ref, out_ref):
    slots, rank, width = lift_ref.shape
    spread = spread_rows(rank_ref[...], slot_ref[...], slots)
    extra = jnp.dot(spread, lift_ref[...].reshape(slots * rank, width), preferred_element_type=F32)
    out_ref[...] = (sum_ref[...] + extra).astype(BF16)


def last_call(slot_row, rank_t, sums, lift):
    return call(
        last_kernel, "last", [IN_VMEM] * 4, jax.ShapeDtypeStruct(sums.shape, BF16), []
    )(slot_row, rank_t, sums, lift)


def after(value, *behind):
    return lax.optimization_barrier((value, *behind))[0]


def swap(value, axis, size, mask):
    return lax.ppermute(value, axis, [(i, i ^ mask) for i in range(size)])


def gather_dp(block, beside):
    me = lax.axis_index("dp")
    chip = me >> 1
    blocks = [block] + [swap(block, "dp", 8, 2 * mask) for mask in (1, 2, 3)]
    blocks, beside = lax.optimization_barrier((blocks, beside))
    other = jnp.stack([swap(one, "dp", 8, 1) for one in blocks])
    near = jnp.stack(blocks)
    both = jnp.where((me & 1) == 0, jnp.stack([near, other], 1), jnp.stack([other, near], 1))
    both = jnp.where((chip & 1) == 0, both, jnp.stack([both[1], both[0], both[3], both[2]]))
    both = jnp.where((chip & 2) == 0, both, jnp.stack([both[2], both[3], both[0], both[1]]))
    return both.reshape(8 * block.shape[0], block.shape[1]), beside


def sum_everywhere(value, beside=()):
    made = []
    for stage, (axis, size, masks) in enumerate(
        (("dp", 8, (1,)), ("dp", 8, (6, 2, 4)), ("tensor", 4, (1,)), ("tensor", 4, (2,)))
    ):
        others = [swap(value, axis, size, mask) for mask in masks]
        for when, work in beside:
            if when == stage:
                made.append(work(value, *made[-1:]))
                others, made[-1] = lax.optimization_barrier((others, made[-1]))
        value = sum(others, value)
    return value, made


def scatter_dp(rows):
    total, width = rows.shape
    me = lax.axis_index("dp")
    core = me & 1
    blocks = rows.reshape(4, 2, total // 8, width)
    mine = lax.dynamic_index_in_dim(blocks, core, 1, keepdims=False)
    other = lax.dynamic_index_in_dim(blocks, 1 - core, 1, keepdims=False)
    both = (mine.astype(F32) + swap(other, "dp", 8, 1).astype(F32)).astype(BF16)
    chip = me >> 1
    kept = lax.dynamic_index_in_dim(both, chip, 0, keepdims=False).astype(F32)
    for mask in (3, 1, 2):
        sent = lax.dynamic_index_in_dim(both, chip ^ mask, 0, keepdims=False)
        kept = kept + swap(sent, "dp", 8, 2 * mask).astype(F32)
    return kept.astype(BF16)


def line_device(
    tokens,
    gate_weight,
    up_weight,
    down_weight,
    adapter_proj_in,
    adapter_lift_in,
    adapter_proj_out,
    adapter_lift_out,
    token_request,
    request_adapter,
    adapter_slot,
):
    slot_of = lookup(lookup(token_request, request_adapter), adapter_slot)
    gathered, slot_of = gather_dp(tokens, slot_of)
    dp_index = lax.axis_index("dp")
    tensor_index = lax.axis_index("tensor")
    side = (tensor_index >> 1).astype(jnp.int32).reshape(1)
    is_end = (tensor_index == 0) | (tensor_index == 3)
    slot_dp = slot_of - dp_index * adapter_proj_in.shape[0]
    slot_tensor = slot_of - tensor_index * adapter_lift_in.shape[0]
    rank_part = rank_in_call(slot_dp[None, :], gathered, adapter_proj_in)
    rank_in, mains = sum_everywhere(
        rank_part,
        [
            (1, lambda tie: main_call(0, CHUNKS[0], after(gathered, tie), gate_weight)),
            (2, lambda tie, before: main_call(0, CHUNKS[0], after(gathered, tie, before), up_weight)),
        ],
    )
    rank_in = rank_in.astype(BF16)
    slot_row = slot_tensor[None, :]
    chunks = len(CHUNKS)
    starts = [sum(CHUNKS[:c]) for c in range(chunks)]
    near, far, hop, hidden_near, hidden_far = ({} for _ in range(5))

    def operand(c, stage):
        if stage == 0:
            return far[c]
        if stage == 1:
            return (far[c].astype(F32) + hop[c].astype(F32)).astype(BF16)
        if stage == 2:
            return (near[c].astype(F32) + hop[c].astype(F32)).astype(BF16)
        if stage == 3:
            both = near[c].astype(F32) + hop[c].astype(F32)
            hidden_near[c] = (jax.nn.silu(both[0]) * both[1]).astype(BF16)[None]
            return hidden_near[c]
        if stage == 4:
            hidden_near[c] = jnp.where(is_end, hidden_near[c], hop[c])
            return hop[c]
        hidden_far[c] = hop[c]
        return hop[c]

    def pair(c):
        return [hidden_near[c][0], jnp.where(is_end, hop[c], hidden_far[c])[0]]

    def padded(value, shape):
        return jnp.pad(value, [(0, b - a) for a, b in zip(value.shape, shape)])

    near[0], far[0], spread = first_call(side, slot_row, rank_in, *mains[:2], adapter_lift_in)
    sums, ranks = None, None
    for slot in range(chunks + 5):
        live = [(slot - stage, stage) for stage in range(6) if 0 <= slot - stage < chunks]
        values = {stage % 3: operand(c, stage) for c, stage in live}
        if 0 in values and 2 in values:
            shape = tuple(max(a, b) for a, b in zip(values[0].shape, values[2].shape))
            outer = jnp.where(is_end, padded(values[0], shape), padded(values[2], shape))
        else:
            outer = values.get(0, values.get(2))
        sent = [value for value in (outer, values.get(1)) if value is not None]
        sent = list(lax.optimization_barrier(tuple(sent)))
        arrived = {}
        if outer is not None:
            arrived[0] = lax.ppermute(sent[0], "tensor", OUTER)
        if 1 in values:
            arrived[1] = lax.ppermute(sent[-1], "tensor", MIDDLE)
        made = ()
        if slot + 1 < chunks:
            ready = False
            made = into_call(
                starts[slot + 1],
                CHUNKS[slot + 1],
                after(side, *sent),
                spread,
                gathered,
                mains[2] if ready else gate_weight,
                up_weight,
                adapter_lift_in,
                ready,
            )
        done = slot - 6
        if done == 0:
            early = pair(0)
            zero = jnp.zeros((adapter_proj_out.shape[1], gathered.shape[0]), F32)
            ranks, _ = project_call(starts[0], 0, 1, after(side, *sent), slot_row, early, adapter_proj_out, zero)
            made = (ranks,)
        elif done > 0:
            ranks, ahead = project_call(
                starts[1], starts[2], CHUNKS[2], after(side, *sent), slot_row, pair(1), adapter_proj_out, ranks
            )
            sums = down_call(starts[0], after(side, ranks), early, down_weight, None)
            made = (ranks, ahead, sums)
        *came, = lax.optimization_barrier((*arrived.values(), *made))
        arrived = dict(zip(arrived, came))
        made = came[len(arrived):]
        if slot + 1 < chunks:
            near[slot + 1], far[slot + 1] = made
        elif done == 0:
            (ranks,) = made
        elif done > 0:
            ranks, ahead, sums = made
        for c, stage in live:
            value = arrived[stage % 3 % 2]
            units, width = (2, 1)[stage // 3], CHUNKS[c] * CELL
            hop[c] = value[:units, :, :width]
    ranks = project_last_call(side, slot_row, pair(2), ahead, ranks)
    rank_out, made = sum_everywhere(
        ranks,
        [
            (2, lambda tie: down_call(starts[1], after(side, tie), pair(1), down_weight, sums)),
            (3, lambda tie, before: down_call(starts[2], after(side, tie), pair(2), down_weight, before)),
        ],
    )
    return scatter_dp(last_call(slot_dp[None, :], rank_out.astype(BF16), made[-1], adapter_lift_out))


def solution(mesh):
    on_line = mesh.shape["tensor"] == 4 and mesh.shape["dp"] == 8
    placed = (
        P("dp", "tensor"),
        P("tensor", "dp"),
        P("tensor", "dp"),
        P("dp", "tensor"),
        P("dp", None, "tensor"),
        P("tensor", None, None, "dp"),
        P("tensor", None, "dp"),
        P("dp", None, "tensor"),
        P(),
        P(),
        P(),
    )
    return jax.shard_map(
        line_device if on_line else general_device, mesh=mesh, in_specs=placed, out_specs=P("dp", "tensor"), check_vma=False
    )
```
